128 devices in a mesh: section: 4 (over x), tensor: 16 (over z, y_lo, core), dp: 2 (over y_hi).
Axes of the slice: x: 4, y: 4 (y_hi: 2, y_lo: 2; y = y_hi * 2 + y_lo), z: 4, core: 2. Of those that a mesh axis runs over, the one named last changes fastest.
Arguments:
- held_input: bfloat16 [4, 2, 2, 64, 12288], P('section', 'dp', None, None, 'tensor'), may hold values from -6 to 6
- query_key: bfloat16 [4, 2, 2, 2, 64, 6144], P('section', 'dp', None, None, None, 'tensor'), may hold values from -4.6 to 4.6, as said below
- w_value: bfloat16 [4, 12288, 6144], P('section', 'dp', 'tensor'), may hold values from -0.0546875 to 0.0546875
- w_out: bfloat16 [4, 12288, 6144], P('section', 'dp', 'tensor'), may hold values from -0.0546875 to 0.0546875
- grad_top: bfloat16 [2, 2, 64, 12288], P('dp', None, None, 'tensor'), may hold values from -6 to 6
- slot_table: int32 [4, 2], replicated, may hold values from 0 to 1, each once within a row
Outputs:
- grad_input: bfloat16 [4, 2, 2, 64, 12288], P('section', 'dp', None, None, 'tensor')
- grad_w_value: bfloat16 [4, 12288, 6144], P('section', 'dp', 'tensor')
- grad_w_out: bfloat16 [4, 12288, 6144], P('section', 'dp', 'tensor')
The draws below stay inside these ranges and needn't reach their ends.
Inputs may be any that keep to these rules, and one draw needn't show every extreme that they name: `query_key`: stashed queries and keys of the heads, kept from the forward pass. `slot_table`: each row is an ordering of the 2 stash slots.
All inputs are finite; a program needn't handle non-finite values.
Results may differ from the reference program's by a relative error of at most 0.04.
Values may be sent and summed in bfloat16 or wider, within the bound.
No kernel may reach another device: no remote copies, remote signals or barrier semaphores. Data moves between devices by JAX's collectives and lax.ppermute only.
A program may use at most 128 MiB of HBM per device.

```python
import jax
import jax.numpy as jnp
from jax import lax

D = 12288
HEADS = 48
DH = 128
SEQ = 64
MICRO = 2
SECTIONS = 4
REPLICAS = 2
HW = 6144
N_TENSOR = 16


def draw_query_key(key, part):
    key = jax.random.fold_in(key, 11)
    key_base = jax.random.fold_in(key, 0)
    full_shape = (SECTIONS, REPLICAS, MICRO, 2, SEQ, HEADS * DH)
    base_draw = jnp.clip(jax.random.normal(key_base, full_shape, jnp.float32), -4.5, 4.5)
    return base_draw.astype(jnp.bfloat16)


def levels(own_key, shape, pieces, smallest, high):
    gain = 1.0
    for axis_at, shards_of in pieces:
        heights = jax.random.uniform(jax.random.fold_in(jax.random.fold_in(own_key, 6), axis_at), (shards_of,), jnp.float32, smallest / len(pieces), high / len(pieces))
        gain = gain * jnp.repeat(jnp.exp(heights), shape[axis_at] // shards_of).reshape((-1,) + (1,) * (len(shape) - 1 - axis_at))
    return gain


def bell_draw(key, shape, scale, reach, cuts=(), kind=jnp.bfloat16):
    level = levels(key, shape, cuts, -0.22, 0.18) if cuts else 1.0
    drawn = jax.random.normal(key, shape, jnp.float32) * scale * level
    return jnp.minimum(jnp.maximum(drawn, -reach), reach).astype(kind)


def setup_inputs(seed: int = 0) -> dict:
    keys = jax.random.split(jax.random.key(seed), 7)
    return {
        "held_input": bell_draw(keys[0], (SECTIONS, REPLICAS, MICRO, SEQ, D), 1.0, 6.0, ((0, 4), (1, 2), (4, 16))),
        "query_key": draw_query_key(jax.random.fold_in(keys[6], 71), 0),
        "w_value": bell_draw(keys[2], (SECTIONS, D, HW), D ** -0.5, 0.0546875, ((0, 4), (1, 2), (2, 16))),
        "w_out": bell_draw(keys[3], (SECTIONS, D, HW), D ** -0.5, 0.0546875, ((0, 4), (1, 2), (2, 16))),
        "grad_top": bell_draw(keys[4], (REPLICAS, MICRO, SEQ, D), 1.0, 6.0, ((0, 2), (3, 16))),
        "slot_table": jax.vmap(lambda own: jax.random.permutation(own, MICRO))(jax.random.split(keys[5], SECTIONS)).reshape((SECTIONS, MICRO)).astype(jnp.int32),
    }


def settle(array):
    return lax.optimization_barrier(array.astype(jnp.bfloat16)).astype(jnp.float32)


def attention_probs(queries, keys_all):
    scores = jnp.einsum("rmqhe,rmkhe->rmhqk", queries, keys_all) * (DH ** -0.5)
    places = jnp.arange(SEQ)
    causal = places[None, :] <= places[:, None]
    scores = jnp.where(causal, scores, -jnp.inf)
    row_top = jnp.max(scores, axis=-1, keepdims=True)
    weights = jnp.exp(scores - row_top)
    return weights / jnp.sum(weights, axis=-1, keepdims=True)


def reference(held_input, query_key, w_value, w_out, grad_top, slot_table):
    group_cols = HEADS * DH // N_TENSOR
    grad_now = grad_top
    input_list = []
    value_list = []
    out_list = []
    for section_num in range(SECTIONS - 1, -1, -1):
        held_now = held_input[SECTIONS - 1 - section_num]
        layer_in = jnp.take(held_now, slot_table[section_num], axis=1)
        layer_wide = layer_in.astype(jnp.float32)
        value_w = w_value[section_num].astype(jnp.float32)
        out_w = w_out[section_num].astype(jnp.float32)
        values = settle(jnp.einsum("rmsd,dc->rmsc", layer_wide, value_w))
        query_pair = query_key[section_num].astype(jnp.float32)
        queries = query_pair[:, :, 0].reshape(REPLICAS, MICRO, SEQ, HEADS, DH)
        keys_all = query_pair[:, :, 1].reshape(REPLICAS, MICRO, SEQ, HEADS, DH)
        attn_probs = settle(attention_probs(queries, keys_all))
        heads_out = settle(jnp.einsum("rmhqk,rmkhe->rmqhe", attn_probs, values.reshape(REPLICAS, MICRO, SEQ, HEADS, DH)))
        heads_out = heads_out.reshape(REPLICAS, MICRO, SEQ, HEADS * DH)
        grad_wide = grad_now.astype(jnp.float32)
        grad_heads = settle(jnp.einsum("rmsd,dc->rmsc", grad_wide, out_w))
        grad_values = settle(jnp.einsum("rmhqk,rmqhe->rmkhe", attn_probs, grad_heads.reshape(REPLICAS, MICRO, SEQ, HEADS, DH)))
        grad_values = grad_values.reshape(REPLICAS, MICRO, SEQ, HEADS * DH)
        grouped = grad_values.reshape(REPLICAS, MICRO, SEQ, N_TENSOR, group_cols)
        weight_groups = value_w.reshape(D, N_TENSOR, group_cols)
        partial_sums = settle(jnp.einsum("rmsng,dng->rmsnd", grouped, weight_groups))
        branch = jnp.sum(partial_sums, axis=3)
        grad_in = (grad_wide + branch).astype(jnp.bfloat16)
        replica_out = settle(jnp.einsum("rmsd,rmsc->rdc", grad_wide, heads_out))
        replica_value = settle(jnp.einsum("rmsd,rmsc->rdc", layer_wide, grad_values))
        out_list.append(jnp.sum(replica_out, axis=0).astype(jnp.bfloat16))
        value_list.append(jnp.sum(replica_value, axis=0).astype(jnp.bfloat16))
        input_list.append(grad_in)
        grad_now = grad_in
    grad_input = jnp.stack(input_list[::-1], axis=0)
    grad_w_value = jnp.stack(value_list[::-1], axis=0)
    grad_w_out = jnp.stack(out_list[::-1], axis=0)
    return (grad_input, grad_w_value, grad_w_out)
```

```python
import jax
import jax.numpy as jnp
from jax import lax
from jax.experimental import pallas as pl
from jax.experimental.pallas import tpu as pltpu
from jax.sharding import PartitionSpec as P

DH = 128
ALL = ("section", "tensor", "dp")
NZ = 4
F32 = jnp.float32
BF16 = jnp.bfloat16


def place(t):
    return t // 4, (t // 2) % 2, t % 2


def index(z, y, c):
    return (z % NZ) * 4 + y * 2 + c


def in_group(value, dz=0, dy=0, dc=0):
    route = []
    for t in range(4 * NZ):
        z, y, c = place(t)
        route.append((t, index(z + dz, y ^ dy, c ^ dc)))
    return lax.ppermute(value, "tensor", route)


def over_all(value, target):
    sections, n_tensor, n_dp = (lax.axis_size(a) for a in ALL)
    route = []
    for s in range(sections):
        for t in range(n_tensor):
            for d in range(n_dp):
                ts, tt, td = target(s, t, d)
                route.append(((s * n_tensor + t) * n_dp + d, (ts * n_tensor + tt) * n_dp + td))
    return lax.ppermute(value, ALL, route)


def swap_dp(value):
    return lax.ppermute(value, "dp", [(0, 1), (1, 0)])


def to_home(value, dp_id, t_id, new_section, dy=0):
    own = value.shape[-1] // 2
    left, right = value[..., :own], value[..., own:]
    got = []
    for j in range(2):
        chosen = jnp.where(dp_id == j, left, right)

        def target(s, t, d, j=j):
            b = 2 * t + (j ^ d)
            return new_section(s), (b % 16) ^ (dy << 1), b // 16

        got.append(over_all(chosen, target))
    even = t_id % 2 == 0
    return jnp.stack([jnp.where(even, got[0], got[1]), jnp.where(even, got[1], got[0])])


def from_home(value, dp_id, t_id, new_section):
    even = t_id % 2 == 0
    got = []
    for j in range(2):
        chosen = jnp.where(even, value[j], value[1 - j])

        def target(s, t, d, j=j):
            return new_section(s), (16 * d + t) // 2, j ^ (t % 2)

        got.append(over_all(chosen, target))
    first = dp_id == 0
    return jnp.concatenate(
        [jnp.where(first, got[0], got[1]), jnp.where(first, got[1], got[0])], axis=-1
    )


def reorder_kernel(order, w_ref, o_ref):
    o_ref[...] = w_ref[...]


def reorder(weights, order):
    n = order.shape[0]
    rows, cols = weights.shape
    own = rows // 16
    return pl.pallas_call(
        reorder_kernel,
        grid_spec=pltpu.PrefetchScalarGridSpec(
            num_scalar_prefetch=1,
            grid=(n,),
            in_specs=[pl.BlockSpec((own, cols), lambda i, o: (o[i], 0))],
            out_specs=pl.BlockSpec((own, cols), lambda i, o: (i, 0)),
        ),
        out_shape=jax.ShapeDtypeStruct((n * own, cols), weights.dtype),
        cost_estimate=pl.CostEstimate(
            flops=0, bytes_accessed=4 * n * own * cols, transcendentals=0
        ),
    )(order, weights)


def outer_kernel(order, g_ref, h_ref, o_ref):
    o_ref[...] = lax.dot_general(
        g_ref[...], h_ref[...], (((0,), (0,)), ((), ())), preferred_element_type=F32
    ).astype(o_ref.dtype)


def outer(grads, heads, order):
    tokens, width = grads.shape
    cols = heads.shape[1]
    own = width // 16
    return pl.pallas_call(
        outer_kernel,
        grid_spec=pltpu.PrefetchScalarGridSpec(
            num_scalar_prefetch=1,
            grid=(16,),
            in_specs=[
                pl.BlockSpec((tokens, own), lambda i, o: (0, i)),
                pl.BlockSpec((tokens, cols), lambda i, o: (0, 0)),
            ],
            out_specs=pl.BlockSpec((own, cols), lambda i, o: (o[i], 0)),
        ),
        out_shape=jax.ShapeDtypeStruct((width, cols), BF16),
        cost_estimate=pl.CostEstimate(
            flops=2 * tokens * width * cols,
            bytes_accessed=2 * (tokens * width + width * cols),
            transcendentals=0,
        ),
    )(order, grads, heads)


def dot(a, b):
    return jnp.dot(a, b, preferred_element_type=F32)


def dot_t(a, b):
    return lax.dot_general(a, b, (((1,), (1,)), ((), ())), preferred_element_type=F32)


def on_device(held_input, query_key, w_value, w_out, grad_top, slot_table):
    sections = lax.axis_size("section")
    section_id = lax.axis_index("section")
    t_id = lax.axis_index("tensor")
    dp_id = lax.axis_index("dp")
    z, y, c = place(t_id)
    micro, seq, two_own = held_input.shape[2:]
    own = two_own // 2
    local_cols = w_value.shape[2]
    heads = local_cols // DH
    rows = 2 * seq

    order = jnp.stack(
        [
            index(z - k + NZ, y ^ dy, c ^ dc)
            for dc in range(2)
            for k in range(NZ)
            for dy in range(2)
        ]
    ).astype(jnp.int32)
    half = order.shape[0] // 2
    out_near, out_far = reorder(w_out[0], order[:half]), reorder(w_out[0], order[half:])
    value_near, value_far = reorder(w_value[0], order[:half]), reorder(w_value[0], order[half:])

    query_pair = query_key[0, 0]
    queries = query_pair[:, 0].reshape(micro, seq, heads, DH)
    keys_all = query_pair[:, 1].reshape(micro, seq, heads, DH)
    scores = jnp.einsum("mqhe,mkhe->mhqk", queries, keys_all, preferred_element_type=F32)
    scores = scores * DH ** (-0.5)
    places = jnp.arange(seq)
    scores = jnp.where(places[None, :] <= places[:, None], scores, -jnp.inf)
    weights = jnp.exp(scores - jnp.max(scores, axis=-1, keepdims=True))
    probs = (weights / jnp.sum(weights, axis=-1, keepdims=True)).astype(BF16)
    probs_there = swap_dp(probs)
    first = dp_id == 0
    probs = jnp.stack(
        [jnp.where(first, probs, probs_there), jnp.where(first, probs_there, probs)], axis=1
    )

    tops = []
    for m in range(micro):
        pair = [to_home(grad_top[0, m], dp_id, t_id, lambda s: s, dy) for dy in range(2)]
        tops.append(jnp.concatenate(pair, axis=-1).reshape(rows, two_own))

    slot_row = lax.dynamic_index_in_dim(slot_table, sections - 1 - section_id, 0, keepdims=False)
    ordered = jnp.take(held_input[0, 0], slot_row, axis=0)
    stash = to_home(ordered, dp_id, t_id, lambda s: sections - 1 - s)
    stash = jnp.swapaxes(stash, 0, 1).reshape(micro * rows, own)
    layer_in = lax.all_gather(stash, "tensor", axis=1, tiled=True)
    values = dot(layer_in, w_value[0]).astype(BF16)
    values = (values.astype(F32) + swap_dp(values).astype(F32)).astype(BF16)
    heads_out = jnp.einsum(
        "mrhqk,mrkhe->mrqhe",
        probs,
        values.reshape(micro, 2, seq, heads, DH),
        preferred_element_type=F32,
    )
    heads_out = heads_out.astype(BF16).reshape(micro * rows, local_cols)

    is_top = section_id == sections - 1
    tick_total = micro + sections - 1
    received = jnp.zeros((rows, two_own), BF16)
    grads_seen, values_seen, inputs_seen = [], [], []
    for tick in range(tick_total):
        micro_pos = tick - (sections - 1 - section_id)
        position = jnp.clip(micro_pos, 0, micro - 1)
        incoming = jnp.where(is_top, tops[min(tick, micro - 1)], received)
        near = jnp.concatenate(
            [incoming] + [in_group(incoming, dz=k) for k in range(1, NZ)], axis=1
        )
        far = in_group(near, dc=1)
        grads_seen.append(jnp.concatenate([near, far], axis=1))
        grad_heads = (dot(near, out_near) + dot(far, out_far)).astype(BF16)
        grad_heads = (grad_heads.astype(F32) + swap_dp(grad_heads).astype(F32)).astype(BF16)
        probs_now = lax.dynamic_index_in_dim(probs, position, 0, keepdims=False)
        grad_vals = jnp.einsum(
            "rhqk,rqhe->rkhe",
            probs_now,
            grad_heads.reshape(2, seq, heads, DH),
            preferred_element_type=F32,
        )
        grad_vals = grad_vals.astype(BF16).reshape(rows, local_cols)
        values_seen.append(grad_vals)
        from_core = in_group(dot_t(grad_vals, value_far).astype(BF16), dc=1)
        total = dot_t(grad_vals, value_near) + from_core.astype(F32)
        pieces = total.astype(BF16)
        branch = total[:, :two_own]
        for k in range(1, NZ):
            piece = pieces[:, k * two_own : (k + 1) * two_own]
            branch = branch + in_group(piece, dz=-k).astype(F32)
        kept = branch[:, :own] + incoming[:, :own].astype(F32)
        sent = jnp.concatenate([kept, branch[:, own:]], axis=1).astype(BF16)
        straight = over_all(sent, lambda s, t, d: ((s - 1) % sections, t, d)).astype(F32)
        across = over_all(sent, lambda s, t, d: ((s - 1) % sections, t ^ 2, d)).astype(F32)
        across = jnp.concatenate([across[:, own:], across[:, :own]], axis=1)
        received = (straight + across).astype(BF16)
        inputs_seen.append(received[:, :own])

    def of_section(seen, section):
        picks = []
        for m in range(micro):
            picks.append(lax.select_n(section, *[seen[sections - 1 - s + m] for s in range(sections)]))
        return jnp.stack(picks)

    grads = of_section(grads_seen, section_id).reshape(micro * rows, 16 * own)
    value_grads = of_section(values_seen, section_id).reshape(micro * rows, local_cols)
    grad_w_out = outer(grads, heads_out, order)
    grad_w_value = lax.dot_general(
        layer_in, value_grads, (((0,), (0,)), ((), ())), preferred_element_type=F32
    ).astype(BF16)

    done = of_section(inputs_seen, (section_id + 1) % sections).reshape(micro, 2, seq, own)
    grad_input = from_home(jnp.swapaxes(done, 0, 1), dp_id, t_id, lambda s: (s + 1) % sections)
    return grad_input[None, None], grad_w_value[None], grad_w_out[None]


def solution(mesh):
    return jax.shard_map(
        on_device,
        mesh=mesh,
        in_specs=(
            P("section", "dp", None, None, "tensor"),
            P("section", "dp", None, None, None, "tensor"),
            P("section", "dp", "tensor"),
            P("section", "dp", "tensor"),
            P("dp", None, None, "tensor"),
            P(),
        ),
        out_specs=(
            P("section", "dp", None, None, "tensor"),
            P("section", "dp", "tensor"),
            P("section", "dp", "tensor"),
        ),
        check_vma=False,
    )
```

```python
import functools

import jax
import jax.numpy as jnp
from jax import lax
from jax.experimental import pallas as pl
from jax.experimental.pallas import tpu as pltpu
from jax.sharding import PartitionSpec as P

DH = 128
ALL = ("section", "tensor", "dp")
NZ = 4
F32 = jnp.float32
BF16 = jnp.bfloat16


def place(t):
    return t // 4, (t // 2) % 2, t % 2


def index(z, y, c):
    return z * 4 + y * 2 + c


def in_group(value, dz=0, dy=0, dc=0):
    route = []
    for t in range(4 * NZ):
        z, y, c = place(t)
        route.append((t, index(z ^ dz, y ^ dy, c ^ dc)))
    return lax.ppermute(value, "tensor", route)


def over_all(value, target):
    sections, n_tensor, n_dp = (lax.axis_size(a) for a in ALL)
    route = []
    for s in range(sections):
        for t in range(n_tensor):
            for d in range(n_dp):
                ts, tt, td = target(s, t, d)
                if ts >= 0:
                    here = (s * n_tensor + t) * n_dp + d
                    route.append((here, (ts * n_tensor + tt) * n_dp + td))
    return lax.ppermute(value, ALL, route)


def swap_dp(value):
    return lax.ppermute(value, "dp", [(0, 1), (1, 0)])


def to_home(value, dp_id, t_id, new_section, dy=0):
    own = value.shape[-1] // 2
    left, right = value[..., :own], value[..., own:]
    got = []
    for j in range(2):
        chosen = jnp.where(dp_id == j, left, right)

        def target(s, t, d, j=j):
            b = 2 * t + (j ^ d)
            return new_section(s), (b % 16) ^ (dy << 1), b // 16

        got.append(over_all(chosen, target))
    even = t_id % 2 == 0
    return jnp.stack([jnp.where(even, got[0], got[1]), jnp.where(even, got[1], got[0])])


def from_home(value, dp_id, t_id, new_section):
    even = t_id % 2 == 0
    got = []
    for j in range(2):
        chosen = jnp.where(even, value[j], value[1 - j])

        def target(s, t, d, j=j):
            return new_section(s), (16 * d + t) // 2, j ^ (t % 2)

        got.append(over_all(chosen, target))
    first = dp_id == 0
    return jnp.concatenate(
        [jnp.where(first, got[0], got[1]), jnp.where(first, got[1], got[0])], axis=-1
    )


def outer_kernel(order, near_ref, far_ref, h_ref, o_ref, held, sems):
    own = near_ref.shape[1] // 8
    heads = h_ref[...]
    copies = []
    for i in range(16):
        half = near_ref if i < 8 else far_ref
        block = half[:, i % 8 * own : (i % 8 + 1) * own]
        held[i] = lax.dot_general(
            block, heads, (((0,), (0,)), ((), ())), preferred_element_type=F32
        ).astype(held.dtype)
        start = pl.multiple_of(order[i] * own, own)
        copy = pltpu.make_async_copy(held.at[i], o_ref.at[pl.ds(start, own)], sems.at[i])
        copy.start()
        copies.append(copy)
    for copy in copies:
        copy.wait()


def outer(near, far, heads, order):
    tokens, width = near.shape
    cols = heads.shape[1]
    own = width // 8
    vmem = pl.BlockSpec(memory_space=pltpu.VMEM)
    return pl.pallas_call(
        outer_kernel,
        in_specs=[pl.BlockSpec(memory_space=pltpu.SMEM), vmem, vmem, vmem],
        out_specs=pl.BlockSpec(memory_space=pl.ANY),
        out_shape=jax.ShapeDtypeStruct((2 * width, cols), BF16),
        scratch_shapes=[pltpu.VMEM((16, own, cols), BF16), pltpu.SemaphoreType.DMA((16,))],
        compiler_params=pltpu.CompilerParams(vmem_limit_bytes=24 * 1024 * 1024),
        cost_estimate=pl.CostEstimate(
            flops=4 * tokens * width * cols,
            bytes_accessed=4 * (tokens * width + width * cols),
            transcendentals=0,
        ),
    )(order, near, far, heads)


def probs_kernel(qk_ref, o_ref):
    micro, n_heads, seq, _ = o_ref.shape
    query = lax.broadcasted_iota(jnp.int32, (seq, seq), 0)
    key = lax.broadcasted_iota(jnp.int32, (seq, seq), 1)
    for m in range(micro):
        for h in range(n_heads):
            at = slice(h * DH, (h + 1) * DH)
            scores = lax.dot_general(
                qk_ref[m, 0, :, at],
                qk_ref[m, 1, :, at],
                (((1,), (1,)), ((), ())),
                preferred_element_type=F32,
            )
            scores = jnp.where(key <= query, scores * DH ** (-0.5), -jnp.inf)
            weights = jnp.exp(scores - jnp.max(scores, axis=-1, keepdims=True))
            weights = weights / jnp.sum(weights, axis=-1, keepdims=True)
            o_ref[m, h] = weights.astype(o_ref.dtype)


def attention_probs(query_key):
    micro, _, seq, cols = query_key.shape
    return pl.pallas_call(
        probs_kernel,
        out_shape=jax.ShapeDtypeStruct((micro, cols // DH, seq, seq), BF16),
        cost_estimate=pl.CostEstimate(
            flops=2 * micro * seq * seq * cols,
            bytes_accessed=2 * query_key.size,
            transcendentals=micro * cols // DH * seq * seq,
        ),
    )(query_key)


def heads_kernel(turned, n_micro, position, mine_ref, there_ref, probs_ref, o_ref):
    total = (mine_ref[...].astype(F32) + there_ref[...].astype(F32)).astype(BF16)
    _, n_rep, n_heads, seq, _ = probs_ref.shape
    for m in range(n_micro):
        for r in range(n_rep):
            for h in range(n_heads):
                rows = slice((m * n_rep + r) * seq, (m * n_rep + r + 1) * seq)
                cols = slice(h * DH, (h + 1) * DH)
                o_ref[rows, cols] = lax.dot_general(
                    probs_ref[position[0] + m, r, h],
                    total[rows, cols],
                    (((0 if turned else 1,), (0,)), ((), ())),
                    preferred_element_type=F32,
                ).astype(o_ref.dtype)


def head_products(mine, there, probs, position, turned):
    n_micro = mine.shape[0] // (probs.shape[1] * probs.shape[3])
    vmem = pl.BlockSpec(memory_space=pltpu.VMEM)
    return pl.pallas_call(
        functools.partial(heads_kernel, turned, n_micro),
        in_specs=[pl.BlockSpec(memory_space=pltpu.SMEM)] + [vmem] * 3,
        out_specs=vmem,
        out_shape=pltpu.VMEM(mine.shape, BF16),
        cost_estimate=pl.CostEstimate(
            flops=2 * mine.size * probs.shape[-1],
            bytes_accessed=6 * mine.size,
            transcendentals=0,
        ),
    )(position, *in_vmem(mine, there, probs))


def in_vmem(*arrays):
    return [pltpu.with_memory_space_constraint(a, pltpu.VMEM) for a in arrays]


def weight_copies(order, own_ref, got_ref, held, sems):
    block = held.shape[1] // 2
    copies = []
    for k in range(NZ):
        group = []
        for y in range(2):
            t = order[2 * k + y]
            at = pl.ds(y * block, block)
            cols = own_ref.shape[1]
            own = own_ref.at[pl.ds(pl.multiple_of(t * block, block), block)]
            got = got_ref.at[pl.ds(pl.multiple_of(t // 2 * block, block), block)]
            sem = sems.at[2 * (2 * k + y)], sems.at[2 * (2 * k + y) + 1]
            group.append(pltpu.make_async_copy(own, held.at[k, at, pl.ds(0, cols)], sem[0]))
            group.append(pltpu.make_async_copy(got, held.at[k, at, pl.ds(cols, cols)], sem[1]))
        copies.append(group)
    return copies


def gather_kernel(order, a0, a1, a2, a3, own_ref, got_ref, keep_ref, give_ref, held, total, sems):
    cols = keep_ref.shape[1]
    copies = weight_copies(order, own_ref, got_ref, held, sems)
    for group in copies:
        for copy in group:
            copy.start()
    for k, a in enumerate((a0, a1, a2, a3)):
        for copy in copies[k]:
            copy.wait()
        term = jnp.dot(a[...], held[k], preferred_element_type=F32)
        if k == 0:
            total[...] = term
        elif k < NZ - 1:
            total[...] += term
        else:
            term = term + total[...]
            keep_ref[...] = term[:, :cols]
            give_ref[...] = term[:, cols:].astype(give_ref.dtype)


def weight_specs(own, got):
    arrays = [pltpu.with_memory_space_constraint(a, pltpu.HBM) for a in (own, got)]
    return arrays, [pl.BlockSpec(memory_space=pl.ANY)] * 2


def gather_product(pieces, own, got, order):
    rows, width = pieces[0].shape
    cols = own.shape[1]
    vmem = pl.BlockSpec(memory_space=pltpu.VMEM)
    weights, specs = weight_specs(own, got)
    return pl.pallas_call(
        gather_kernel,
        in_specs=[pl.BlockSpec(memory_space=pltpu.SMEM)] + [vmem] * 4 + specs,
        out_specs=[vmem] * 2,
        out_shape=[pltpu.VMEM((rows, cols), F32), pltpu.VMEM((rows, cols), BF16)],
        scratch_shapes=[
            pltpu.VMEM((NZ, width, 2 * cols), BF16),
            pltpu.VMEM((rows, 2 * cols), F32),
            pltpu.SemaphoreType.DMA((4 * NZ,)),
        ],
        compiler_params=pltpu.CompilerParams(vmem_limit_bytes=16 * 1024 * 1024),
        cost_estimate=pl.CostEstimate(
            flops=16 * rows * width * cols,
            bytes_accessed=16 * width * cols,
            transcendentals=0,
        ),
    )(order, *in_vmem(*pieces), *weights)


def branch_kernel(order, v_ref, c_ref, own_ref, got_ref, o0, o1, o2, o3, held, sems):
    outs = (o0, o1, o2, o3)
    copies = weight_copies(order, own_ref, got_ref, held, sems)
    turn = (2, 1, 3, 0)
    for k in turn:
        for copy in copies[k]:
            copy.start()
    both = jnp.concatenate([v_ref[...], c_ref[...]], axis=1)
    for k in turn:
        for copy in copies[k]:
            copy.wait()
        outs[k][...] = lax.dot_general(
            both, held[k], (((1,), (1,)), ((), ())), preferred_element_type=F32
        ).astype(BF16)


def branch_product(vals, vals_core, own, got, order):
    rows, cols = vals.shape
    width = own.shape[0] // (2 * NZ)
    vmem = pl.BlockSpec(memory_space=pltpu.VMEM)
    weights, specs = weight_specs(own, got)
    return pl.pallas_call(
        branch_kernel,
        in_specs=[pl.BlockSpec(memory_space=pltpu.SMEM)] + [vmem] * 2 + specs,
        out_specs=[vmem] * 4,
        out_shape=[pltpu.VMEM((rows, width), BF16)] * 4,
        scratch_shapes=[
            pltpu.VMEM((NZ, width, 2 * cols), BF16),
            pltpu.SemaphoreType.DMA((4 * NZ,)),
        ],
        compiler_params=pltpu.CompilerParams(vmem_limit_bytes=16 * 1024 * 1024),
        cost_estimate=pl.CostEstimate(
            flops=16 * rows * width * cols,
            bytes_accessed=16 * width * cols,
            transcendentals=0,
        ),
    )(order, *in_vmem(vals, vals_core), *weights)


def pick_kernel(sections, micro, section, *refs):
    ticks = sections + micro - 1
    grads = refs[: ticks * NZ]
    near_ref, sems = refs[ticks * NZ :]
    rows, width = grads[0].shape
    for s in range(sections):

        @pl.when(section[0] == s)
        def _(s=s):
            copies = []
            for m in range(micro):
                tick = sections - 1 - s + m
                at = pl.ds(m * rows, rows)
                targets = [near_ref.at[at, pl.ds(k * width, width)] for k in range(NZ)]
                for src, dst in zip(grads[tick * NZ : (tick + 1) * NZ], targets):
                    copies.append(pltpu.make_async_copy(src, dst, sems.at[len(copies)]))
            for copy in copies:
                copy.start()
            for copy in copies:
                copy.wait()


def pick(grads, section, sections, micro):
    rows, width = grads[0][0].shape
    flat = [piece for tick in grads for piece in tick]
    return pl.pallas_call(
        functools.partial(pick_kernel, sections, micro),
        in_specs=[pl.BlockSpec(memory_space=pltpu.SMEM)]
        + [pl.BlockSpec(memory_space=pl.ANY)] * len(flat),
        out_specs=pl.BlockSpec(memory_space=pltpu.VMEM),
        out_shape=jax.ShapeDtypeStruct((micro * rows, NZ * width), BF16),
        scratch_shapes=[pltpu.SemaphoreType.DMA((micro * NZ,))],
        cost_estimate=pl.CostEstimate(
            flops=0, bytes_accessed=4 * micro * rows * NZ * width, transcendentals=0
        ),
    )(section, *flat)


def dot(a, b):
    return jnp.dot(a, b, preferred_element_type=F32)


def after(value, *others):
    return lax.optimization_barrier((value, *others))[0]


def on_device(held_input, query_key, w_value, w_out, grad_top, slot_table):
    sections = lax.axis_size("section")
    section_id = lax.axis_index("section")
    t_id = lax.axis_index("tensor")
    dp_id = lax.axis_index("dp")
    z, y, c = place(t_id)
    micro, seq, two_own = held_input.shape[2:]
    own = two_own // 2
    local_cols = w_value.shape[2]
    heads = local_cols // DH
    rows = 2 * seq
    lower = y == 0

    same, other = (to_home(grad_top[0], dp_id, t_id, lambda s: s, dy) for dy in range(2))
    pair = [jnp.where(lower, same, other), jnp.where(lower, other, same)]
    tops = jnp.swapaxes(jnp.concatenate(pair, axis=-1), 0, 1).reshape(micro, rows, two_own)
    top = tops[0]

    order = [index(z ^ k, yy, c) for k in range(NZ) for yy in range(2)]
    order = jnp.stack(order + [t ^ 1 for t in order]).astype(jnp.int32)

    def traded(weights):
        blocks = weights.reshape(8, 2, own, local_cols)
        given = lax.dynamic_index_in_dim(blocks, 1 - c, 1, keepdims=False)
        return in_group(given.reshape(8 * own, local_cols), dc=1)

    out_got = traded(w_out[0])
    value_got = traded(w_value[0])

    probs = attention_probs(query_key[0, 0])
    probs_there = swap_dp(probs)
    first = dp_id == 0
    probs = jnp.stack(
        [jnp.where(first, probs, probs_there), jnp.where(first, probs_there, probs)], axis=1
    )

    is_top = section_id == sections - 1
    tick_total = micro + sections - 1
    incoming = top
    grads_seen, values_seen, inputs_seen = [], [], []
    stash = heads_out = layer_in = None
    for tick in range(tick_total):
        last = tick == tick_total - 1
        position = jnp.clip(tick - (sections - 1 - section_id), 0, micro - 1)
        position = position.astype(jnp.int32).reshape(1)
        near = [incoming] + [in_group(incoming, dz=k) for k in range(1, NZ)]
        grads_seen.append(near)
        keep, give = gather_product(near, w_out[0], out_got, order)
        from_core = in_group(give, dc=1)
        grad_heads = (keep + from_core.astype(F32)).astype(BF16)
        if tick == 1:
            layer_in = lax.all_gather(after(stash, from_core), "tensor", axis=1, tiled=True)
        if tick == 3:
            values = dot(after(layer_in, from_core), w_value[0]).astype(BF16)
            values_there = swap_dp(values)
        if last:
            grads = pick(
                [*grads_seen[:-1], after(near, from_core)],
                section_id.astype(jnp.int32).reshape(1),
                sections,
                micro,
            )
        grad_vals = head_products(grad_heads, swap_dp(grad_heads), probs, position, True)
        values_seen.append(grad_vals)
        pieces = branch_product(
            grad_vals, in_group(grad_vals, dc=1), w_value[0], value_got, order
        )
        arrived = [in_group(pieces[k], dz=k) for k in range(1, NZ)]
        branch = pieces[0].astype(F32)
        for piece in arrived:
            branch = branch + piece.astype(F32)
        if tick == 0:
            slot_row = lax.dynamic_index_in_dim(
                slot_table, sections - 1 - section_id, 0, keepdims=False
            )
            ordered = jnp.take(after(held_input, arrived[0])[0, 0], slot_row, axis=0)
            stash = to_home(ordered, dp_id, t_id, lambda s: sections - 1 - s)
            stash = jnp.swapaxes(stash, 0, 1).reshape(micro * rows, own)
        if tick == 3:
            heads_out = head_products(
                values, after(values_there, arrived[0]), probs, jnp.zeros((1,), jnp.int32), False
            )
        if last:
            far = in_group(after(grads, pieces[0]), dc=1)
            grad_w_out = outer(grads, after(far, arrived[0]), heads_out, order)
            branch = after(branch, grad_w_out)
        branch = branch.astype(BF16)
        across = in_group(branch, dy=1)
        if last:
            value_grads = [
                lax.select_n(section_id, *[values_seen[sections - 1 - s + m] for s in range(sections)])
                for m in range(micro)
            ]
            grad_w_value = lax.dot_general(
                layer_in,
                jnp.concatenate(value_grads, axis=0),
                (((0,), (0,)), ((), ())),
                preferred_element_type=F32,
            ).astype(BF16)
            across = after(across, grad_w_value)
        done = incoming.astype(F32) + branch.astype(F32) + across.astype(F32)
        done = done.astype(BF16)
        inputs_seen.append(jnp.where(lower, done[:, :own], done[:, own:]))
        if not last:
            received = over_all(done, lambda s, t, d: (s - 1, t, d))
            incoming = jnp.where(is_top, tops[1], received)

    grad_input = jnp.stack(
        [
            lax.select_n(section_id, *[inputs_seen[sections - 1 - s + m] for s in range(sections)])
            for m in range(micro)
        ]
    )
    grad_input = jnp.swapaxes(grad_input.reshape(micro, 2, seq, own), 0, 1)
    grad_input = from_home(grad_input, dp_id, t_id, lambda s: s)
    return grad_input[None, None], grad_w_value[None], grad_w_out[None]


def solution(mesh):
    return jax.shard_map(
        on_device,
        mesh=mesh,
        in_specs=(
            P("section", "dp", None, None, "tensor"),
            P("section", "dp", None, None, None, "tensor"),
            P("section", "dp", "tensor"),
            P("section", "dp", "tensor"),
            P("dp", None, None, "tensor"),
            P(),
        ),
        out_specs=(
            P("section", "dp", None, None, "tensor"),
            P("section", "dp", "tensor"),
            P("section", "dp", "tensor"),
        ),
        check_vma=False,
    )
```

```python
import functools

import jax
import jax.numpy as jnp
from jax import lax
from jax.experimental import pallas as pl
from jax.experimental.pallas import tpu as pltpu
from jax.sharding import PartitionSpec as P

DH = 128
ALL = ("section", "tensor", "dp")
NZ = 4
F32 = jnp.float32
BF16 = jnp.bfloat16


def place(t):
    return t // 4, (t // 2) % 2, t % 2


def index(z, y, c):
    return z * 4 + y * 2 + c


def in_group(value, dz=0, dy=0, dc=0):
    route = []
    for t in range(4 * NZ):
        z, y, c = place(t)
        route.append((t, index(z ^ dz, y ^ dy, c ^ dc)))
    return lax.ppermute(value, "tensor", route)


def over_all(value, target):
    sections, n_tensor, n_dp = (lax.axis_size(a) for a in ALL)
    route = []
    for s in range(sections):
        for t in range(n_tensor):
            for d in range(n_dp):
                ts, tt, td = target(s, t, d)
                if ts >= 0:
                    here = (s * n_tensor + t) * n_dp + d
                    route.append((here, (ts * n_tensor + tt) * n_dp + td))
    return lax.ppermute(value, ALL, route)


def swap_dp(value):
    return lax.ppermute(value, "dp", [(0, 1), (1, 0)])


def home_parts(value, dp_id, new_section, dy=0):
    own = value.shape[-1] // 2
    left, right = value[..., :own], value[..., own:]
    got = []
    for j in range(2):
        chosen = jnp.where(dp_id == j, left, right)

        def target(s, t, d, j=j):
            b = 2 * t + (j ^ d)
            return new_section(s), (b % 16) ^ (dy << 1), b // 16

        got.append(over_all(chosen, target))
    return got


def to_home(value, dp_id, t_id, new_section, dy=0):
    got = home_parts(value, dp_id, new_section, dy)
    even = t_id % 2 == 0
    return jnp.stack([jnp.where(even, got[0], got[1]), jnp.where(even, got[1], got[0])])


def from_home(value, dp_id, t_id, new_section):
    even = t_id % 2 == 0
    got = []
    for j in range(2):
        chosen = jnp.where(even, value[j], value[1 - j])

        def target(s, t, d, j=j):
            return new_section(s), (16 * d + t) // 2, j ^ (t % 2)

        got.append(over_all(chosen, target))
    first = dp_id == 0
    return jnp.concatenate(
        [jnp.where(first, got[0], got[1]), jnp.where(first, got[1], got[0])], axis=-1
    )


def call(kernel, arrays, specs, gates, mib=3, **settings):
    n = len(arrays)
    settings["compiler_params"] = pltpu.CompilerParams(vmem_limit_bytes=mib * 2**20)

    def body(*refs):
        kernel(*refs[:n], *refs[n + len(gates) :])

    specs = list(specs) + [pl.BlockSpec(memory_space=pl.ANY)] * len(gates)
    return pl.pallas_call(body, in_specs=specs, **settings)(*arrays, *gates)


VMEM = pl.BlockSpec(memory_space=pltpu.VMEM)
SMEM = pl.BlockSpec(memory_space=pltpu.SMEM)
ANY = pl.BlockSpec(memory_space=pl.ANY)


def cost(flops, bytes_accessed):
    return pl.CostEstimate(flops=flops, bytes_accessed=bytes_accessed, transcendentals=0)


def in_vmem(*arrays):
    return [pltpu.with_memory_space_constraint(a, pltpu.VMEM) for a in arrays]


def in_hbm(*arrays):
    return [pltpu.with_memory_space_constraint(a, pltpu.HBM) for a in arrays]


def given_kernel(core, u_ref, w_ref, u_out, w_out, sems):
    block = u_out.shape[0] // 8
    copies = []
    for ref, out in ((u_ref, u_out), (w_ref, w_out)):
        for i in range(8):
            start = pl.multiple_of((2 * i + 1 - core[0]) * block, block)
            copies.append(
                pltpu.make_async_copy(
                    ref.at[pl.ds(start, block)],
                    out.at[pl.ds(i * block, block)],
                    sems.at[len(copies)],
                )
            )
    for copy in copies:
        copy.start()
    for copy in copies:
        copy.wait()


def given(first, second, core):
    rows, cols = first.shape
    return call(
        given_kernel,
        [core, *in_hbm(first, second)],
        [SMEM, ANY, ANY],
        (),
        out_specs=[VMEM] * 2,
        out_shape=[pltpu.VMEM((rows // 2, cols), BF16)] * 2,
        scratch_shapes=[pltpu.SemaphoreType.DMA((16,))],
        mib=8,
        cost_estimate=cost(0, 4 * rows * cols),
    )


def sum_kernel(y, p_ref, a_ref, b_ref, c_ref, g_ref, o_ref):
    own = o_ref.shape[1] // 2
    total = p_ref[...].astype(F32) + a_ref[...].astype(F32)
    total += b_ref[...].astype(F32) + c_ref[...].astype(F32)
    mine = lax.broadcasted_iota(jnp.int32, total.shape, 1) // own == y[0]
    o_ref[...] = (total + jnp.where(mine, g_ref[...].astype(F32), 0)).astype(BF16)


def z_sum(piece, arrived, grad, y, gates):
    return call(
        sum_kernel,
        [y, *in_vmem(piece, *arrived, grad)],
        [SMEM] + [VMEM] * 5,
        gates,
        out_specs=VMEM,
        out_shape=pltpu.VMEM(piece.shape, BF16),
        cost_estimate=cost(6 * piece.size, 12 * piece.size),
    )


def enter_kernel(at, s_ref, a_ref, t_ref, o_ref, own_ref):
    own = own_ref.shape[1]
    total = (s_ref[...].astype(F32) + a_ref[...].astype(F32)).astype(BF16)
    own_ref[...] = jnp.where(at[0] == 0, total[:, :own], total[:, own:])
    o_ref[...] = jnp.where(at[1] == 1, t_ref[...], total)


def enter(straight, across, top, at, gates):
    rows, width = straight.shape
    return call(
        enter_kernel,
        [at, *in_vmem(straight, across, top)],
        [SMEM] + [VMEM] * 3,
        gates,
        out_specs=[VMEM] * 2,
        out_shape=[
            pltpu.VMEM((rows, width), BF16),
            pltpu.VMEM((rows, width // 2), BF16),
        ],
        cost_estimate=cost(2 * straight.size, 8 * straight.size),
    )


def outer_kernel(order, n0, n1, f0, f1, h_ref, o_ref, held, sems):
    own = n0.shape[1] // 8
    heads = h_ref[...]
    copies = []
    for i in range(16):
        at = slice(i % 8 * own, (i % 8 + 1) * own)
        block = [half[:, at] for half in ((n0, n1) if i < 8 else (f0, f1))]
        held[i] = lax.dot_general(
            jnp.concatenate(block, axis=0),
            heads,
            (((0,), (0,)), ((), ())),
            preferred_element_type=F32,
        ).astype(held.dtype)
        start = pl.multiple_of(order[i] * own, own)
        copy = pltpu.make_async_copy(held.at[i], o_ref.at[pl.ds(start, own)], sems.at[i])
        copy.start()
        copies.append(copy)
    for copy in copies:
        copy.wait()


def outer(near, far, heads, order):
    tokens, cols = heads.shape
    width = near[0].shape[1]
    own = width // 8
    return call(
        outer_kernel,
        [order, *near, *far, heads],
        [SMEM] + [VMEM] * 5,
        (),
        out_specs=ANY,
        out_shape=jax.ShapeDtypeStruct((2 * width, cols), BF16),
        scratch_shapes=[pltpu.VMEM((16, own, cols), BF16), pltpu.SemaphoreType.DMA((16,))],
        mib=10,
        cost_estimate=cost(4 * tokens * width * cols, 4 * (tokens * width + width * cols)),
    )


def slots_kernel(slots, held_ref, o_ref, sems):
    copies = [
        pltpu.make_async_copy(held_ref.at[slots[m]], o_ref.at[m], sems.at[m])
        for m in range(o_ref.shape[0])
    ]
    for copy in copies:
        copy.start()
    for copy in copies:
        copy.wait()


def in_slots(held, slots, gates):
    return call(
        slots_kernel,
        [slots, held],
        [SMEM, ANY],
        gates,
        out_specs=VMEM,
        out_shape=pltpu.VMEM(held.shape, BF16),
        scratch_shapes=[pltpu.SemaphoreType.DMA((held.shape[0],))],
        cost_estimate=cost(0, 4 * held.size),
    )


def stash_kernel(odd, a_ref, b_ref, o_ref):
    even = odd[0] == 0
    micro, seq, _ = a_ref.shape
    for m in range(micro):
        for r, (first, second) in enumerate(((a_ref, b_ref), (b_ref, a_ref))):
            at = slice((2 * m + r) * seq, (2 * m + r + 1) * seq)
            o_ref[at, :] = jnp.where(even, first[m], second[m])


def stash_rows(parts, odd, gates):
    micro, seq, own = parts[0].shape
    return call(
        stash_kernel,
        [odd, *parts],
        [SMEM] + [VMEM] * 2,
        gates,
        out_specs=VMEM,
        out_shape=jax.ShapeDtypeStruct((2 * micro * seq, own), BF16),
        cost_estimate=cost(0, 8 * parts[0].size),
    )


def tie_kernel(x_ref, o_ref):
    pass


def tie(value, *gates):
    return call(
        tie_kernel,
        [value],
        [ANY],
        gates,
        out_specs=ANY,
        out_shape=jax.ShapeDtypeStruct(value.shape, value.dtype),
        input_output_aliases={0: 0},
        cost_estimate=cost(0, 0),
    )


def probs_kernel(qk_ref, o_ref):
    micro, n_heads, seq, _ = o_ref.shape
    query = lax.broadcasted_iota(jnp.int32, (seq, seq), 0)
    key = lax.broadcasted_iota(jnp.int32, (seq, seq), 1)
    for m in range(micro):
        for h in range(n_heads):
            at = slice(h * DH, (h + 1) * DH)
            scores = lax.dot_general(
                qk_ref[m, 0, :, at],
                qk_ref[m, 1, :, at],
                (((1,), (1,)), ((), ())),
                preferred_element_type=F32,
            )
            scores = jnp.where(key <= query, scores * DH ** (-0.5), -jnp.inf)
            weights = jnp.exp(scores - jnp.max(scores, axis=-1, keepdims=True))
            weights = weights / jnp.sum(weights, axis=-1, keepdims=True)
            o_ref[m, h] = weights.astype(o_ref.dtype)


def attention_probs(query_key, gates):
    micro, _, seq, cols = query_key.shape
    return call(
        probs_kernel,
        [query_key],
        [VMEM],
        gates,
        out_specs=VMEM,
        out_shape=jax.ShapeDtypeStruct((micro, cols // DH, seq, seq), BF16),
        cost_estimate=cost(2 * micro * seq * seq * cols, 2 * query_key.size),
    )


def heads_kernel(turned, n_micro, position, mine_ref, there_ref, probs_ref, o_ref):
    total = (mine_ref[...].astype(F32) + there_ref[...].astype(F32)).astype(BF16)
    _, n_rep, n_heads, seq, _ = probs_ref.shape
    for m in range(n_micro):
        for r in range(n_rep):
            for h in range(n_heads):
                rows = slice((m * n_rep + r) * seq, (m * n_rep + r + 1) * seq)
                cols = slice(h * DH, (h + 1) * DH)
                o_ref[rows, cols] = lax.dot_general(
                    probs_ref[position[0] + m, r, h],
                    total[rows, cols],
                    (((0 if turned else 1,), (0,)), ((), ())),
                    preferred_element_type=F32,
                ).astype(o_ref.dtype)


def head_products(mine, there, probs, position, turned, gates):
    n_micro = mine.shape[0] // (probs.shape[1] * probs.shape[3])
    return call(
        functools.partial(heads_kernel, turned, n_micro),
        [position, *in_vmem(mine, there, probs)],
        [SMEM] + [VMEM] * 3,
        gates,
        out_specs=VMEM,
        out_shape=pltpu.VMEM(mine.shape, BF16),
        cost_estimate=cost(2 * mine.size * probs.shape[-1], 6 * mine.size),
    )


def weight_copies(order, own_ref, got_ref, held, sems):
    block = held.shape[1] // 2
    copies = []
    for k in range(NZ):
        group = []
        for y in range(2):
            t = order[2 * k + y]
            at = pl.ds(y * block, block)
            cols = own_ref.shape[1]
            own = own_ref.at[pl.ds(pl.multiple_of(t * block, block), block)]
            got = got_ref.at[pl.ds(pl.multiple_of(t // 2 * block, block), block)]
            sem = sems.at[2 * (2 * k + y)], sems.at[2 * (2 * k + y) + 1]
            group.append(pltpu.make_async_copy(own, held.at[k, at, pl.ds(0, cols)], sem[0]))
            group.append(pltpu.make_async_copy(got, held.at[k, at, pl.ds(cols, cols)], sem[1]))
        copies.append(group)
    return copies


def load_kernel(turned, order, own_ref, got_ref, o_ref, *scratch):
    held = scratch[0] if turned else o_ref
    copies = weight_copies(order, own_ref, got_ref, held, scratch[-1])
    for group in copies:
        for copy in group:
            copy.start()
    for k, group in enumerate(copies):
        for copy in group:
            copy.wait()
        if turned:
            o_ref[k] = held[k].T


def load(own, got, order, turned, gates):
    width, cols = own.shape[0] // (2 * NZ), 2 * own.shape[1]
    held = [pltpu.VMEM((NZ, width, cols), BF16)] if turned else []
    shape = (NZ, cols, width) if turned else (NZ, width, cols)
    return call(
        functools.partial(load_kernel, turned),
        [order, *in_hbm(own, got)],
        [SMEM, ANY, ANY],
        gates,
        out_specs=VMEM,
        out_shape=pltpu.VMEM(shape, BF16),
        scratch_shapes=held + [pltpu.SemaphoreType.DMA((4 * NZ,))],
        mib=11 if turned else 6,
        cost_estimate=cost(0, 8 * NZ * width * cols),
    )


def gather_kernel(a0, a1, a2, a3, w_ref, keep_ref, give_ref, total):
    cols = keep_ref.shape[1]
    for k, a in enumerate((a0, a1, a2, a3)):
        term = jnp.dot(a[...], w_ref[k], preferred_element_type=F32)
        if k == 0:
            total[...] = term
        elif k < NZ - 1:
            total[...] += term
        else:
            term = term + total[...]
            keep_ref[...] = term[:, :cols]
            give_ref[...] = term[:, cols:].astype(give_ref.dtype)


def gather_product(pieces, weights, gates):
    rows, width = pieces[0].shape
    cols = weights.shape[2] // 2
    return call(
        gather_kernel,
        in_vmem(*pieces, weights),
        [VMEM] * 5,
        gates,
        out_specs=[VMEM] * 2,
        out_shape=[pltpu.VMEM((rows, cols), F32), pltpu.VMEM((rows, cols), BF16)],
        scratch_shapes=[pltpu.VMEM((rows, 2 * cols), F32)],
        mib=3,
        cost_estimate=cost(16 * rows * width * cols, 16 * width * cols),
    )


def branch_kernel(v_ref, c_ref, w_ref, o0, o1, o2, o3):
    both = jnp.concatenate([v_ref[...], c_ref[...]], axis=1)
    for k, out in enumerate((o0, o1, o2, o3)):
        out[...] = jnp.dot(both, w_ref[k], preferred_element_type=F32).astype(BF16)


def branch_product(vals, vals_core, weights):
    rows, cols = vals.shape
    width = weights.shape[2]
    return call(
        branch_kernel,
        in_vmem(vals, vals_core, weights),
        [VMEM] * 3,
        (),
        out_specs=[VMEM] * 4,
        out_shape=[pltpu.VMEM((rows, width), BF16)] * 4,
        mib=3,
        cost_estimate=cost(16 * rows * width * cols, 16 * width * cols),
    )


def pick_kernel(section, *refs):
    grads, near_ref, sems = refs[:-2], *refs[-2:]
    n = sems.shape[0]
    sections = len(grads) // n
    width = grads[0].shape[1]
    for s in range(sections):

        @pl.when(section[0] == s)
        def _(s=s):
            copies = []
            for k in range(n):
                copies.append(
                    pltpu.make_async_copy(
                        grads[s * n + k], near_ref.at[:, pl.ds(k * width, width)], sems.at[k]
                    )
                )
            for copy in copies:
                copy.start()
            for copy in copies:
                copy.wait()


def pick(grads, section, gates, n=NZ):
    rows, width = grads[0][0].shape
    flat = [piece for entry in grads for piece in entry]
    return call(
        pick_kernel,
        [section, *flat],
        [SMEM] + [ANY] * len(flat),
        gates,
        out_specs=VMEM,
        out_shape=pltpu.VMEM((rows, n * width), BF16),
        scratch_shapes=[pltpu.SemaphoreType.DMA((n,))],
        cost_estimate=cost(0, 4 * rows * n * width),
    )


def pick_one(seen, section, gates):
    return pick([[one] for one in seen], section, gates, 1)


def dot(a, b):
    return jnp.dot(a, b, preferred_element_type=F32)


def on_device(held_input, query_key, w_value, w_out, grad_top, slot_table):
    sections = lax.axis_size("section")
    section_id = lax.axis_index("section")
    t_id = lax.axis_index("tensor")
    dp_id = lax.axis_index("dp")
    z, y, c = place(t_id)
    micro, seq, two_own = held_input.shape[2:]
    own = two_own // 2
    local_cols = w_value.shape[2]
    heads = local_cols // DH
    rows = 2 * seq
    lower = y == 0

    same, other = (to_home(grad_top[0], dp_id, t_id, lambda s: s, dy) for dy in range(2))
    pair = [jnp.where(lower, same, other), jnp.where(lower, other, same)]
    tops = jnp.swapaxes(jnp.concatenate(pair, axis=-1), 0, 1).reshape(micro, rows, two_own)
    top = tops[0]

    order = [index(z ^ k, yy, c) for k in range(NZ) for yy in range(2)]
    order = jnp.stack(order + [t ^ 1 for t in order]).astype(jnp.int32)

    core = c.astype(jnp.int32).reshape(1)
    section = section_id.astype(jnp.int32).reshape(1)
    at = jnp.stack([y, section_id == sections - 1]).astype(jnp.int32)

    out_given, value_given = given(w_out[0], w_value[0], core)
    out_got = in_group(out_given, dc=1)
    value_got = in_group(value_given, dc=1)

    probs = attention_probs(query_key[0, 0], (out_got,))
    probs_there = swap_dp(probs)
    first = dp_id == 0
    probs = jnp.stack(
        [jnp.where(first, probs, probs_there), jnp.where(first, probs_there, probs)], axis=1
    )

    tick_total = micro + sections - 1
    incoming = top
    out_ready = load(w_out[0], out_got, order, False, ())
    grads_seen, values_seen, inputs_seen = [], [], []
    stash = values = values_there = heads_out = layer_in = None

    def chosen(seen):
        return lax.select_n(section_id, *seen)

    for tick in range(tick_total):
        last = tick == tick_total - 1
        position = jnp.clip(tick - (sections - 1 - section_id), 0, micro - 1)
        position = position.astype(jnp.int32).reshape(1)
        near = [incoming] + [in_group(incoming, dz=k) for k in range(1, NZ)]
        grads_seen.append(near)
        gates = ()
        if tick == 1:
            stash = stash_rows(stash, c.astype(jnp.int32).reshape(1), (incoming,))
            layer_in = lax.all_gather(stash, "tensor", axis=1, tiled=True)
        if last:
            first_grads = pick(grads_seen[:sections][::-1], section, (incoming,))
            ends = [
                pick_one(
                    [
                        inputs_seen[min(sections - 1 - (s + 1) % sections + m, tick - 1)]
                        for s in range(sections)
                    ],
                    section,
                    (incoming,),
                )
                for m in range(micro)
            ]
            early = from_home(
                jnp.stack([end.reshape(2, seq, own) for end in ends], axis=1),
                dp_id,
                t_id,
                lambda s: (s + 1) % sections,
            )
            first_values = pick_one(values_seen[::-1], section, (incoming,))
            gates = (first_grads, first_values, *ends)
        keep, give = gather_product(near, out_ready, gates)
        from_core = in_group(give, dc=1)
        grad_heads = (keep + from_core.astype(F32)).astype(BF16)
        there = swap_dp(grad_heads)
        value_ready = load(w_value[0], value_got, order, True, (grad_heads,))
        gates = (value_ready,)
        if tick == 3:
            heads_out = head_products(
                values, values_there, probs, jnp.zeros((1,), jnp.int32), False, (grad_heads,)
            )
            gates += (heads_out,)
        if last:
            later_grads = pick(grads_seen[1:][::-1], section, (grad_heads,))
            gates += (later_grads,)
        grad_vals = head_products(grad_heads, there, probs, position, True, gates)
        values_seen.append(grad_vals)
        pieces = branch_product(grad_vals, in_group(grad_vals, dc=1), value_ready)
        arrived = [in_group(pieces[k], dz=k) for k in range(1, NZ)]
        gates = ()
        if last:
            far = [
                in_group(tie(picked, pieces[0]), dc=1) for picked in (first_grads, later_grads)
            ]
            grad_w_out = outer([first_grads, later_grads], far, heads_out, order)
            later_values = pick_one(values_seen[1:][::-1], section, (pieces[0],))
            grad_w_value = lax.dot_general(
                layer_in,
                jnp.concatenate([first_values, later_values], axis=0),
                (((0,), (0,)), ((), ())),
                preferred_element_type=F32,
            ).astype(BF16)
            gates = (grad_w_value, grad_w_out)
        sent = z_sum(pieces[0], arrived, incoming, at[:1], gates)
        if tick == 0:
            slot_row = lax.dynamic_index_in_dim(
                slot_table, sections - 1 - section_id, 0, keepdims=False
            )
            ordered = in_slots(held_input[0, 0], slot_row, (sent,))
            stash = home_parts(ordered, dp_id, lambda s: sections - 1 - s)
        if last:
            across = in_group(sent, dy=1)
            _, done = enter(sent, across, sent, at, ())
        else:
            straight = over_all(sent, lambda s, t, d: ((s - 1) % sections, t, d))
            across = over_all(sent, lambda s, t, d: ((s - 1) % sections, t ^ 2, d))
            out_ready = load(w_out[0], out_got, order, False, (sent,))
            gates = ()
            if tick == 2:
                values = dot(layer_in, w_value[0]).astype(BF16)
                values_there = swap_dp(values)
                gates = (values,)
            incoming, completed = enter(straight, across, tops[1], at, gates)
            inputs_seen.append(completed)

    late = from_home(done.reshape(2, seq, own), dp_id, t_id, lambda s: s if s == 0 else -1)
    late = jnp.where(section_id == 0, late, early[micro - 1])
    grad_input = jnp.stack([*early[: micro - 1], late])
    return grad_input[None, None], grad_w_value[None], grad_w_out[None]


def solution(mesh):
    return jax.shard_map(
        on_device,
        mesh=mesh,
        in_specs=(
            P("section", "dp", None, None, "tensor"),
            P("section", "dp", None, None, None, "tensor"),
            P("section", "dp", "tensor"),
            P("section", "dp", "tensor"),
            P("dp", None, None, "tensor"),
            P(),
        ),
        out_specs=(
            P("section", "dp", None, None, "tensor"),
            P("section", "dp", "tensor"),
            P("section", "dp", "tensor"),
        ),
        check_vma=False,
    )
```

```python
import functools

import jax
import jax.numpy as jnp
from jax import lax
from jax.experimental import pallas as pl
from jax.experimental.pallas import tpu as pltpu
from jax.sharding import PartitionSpec as P

DH = 128
ALL = ("section", "tensor", "dp")
NZ = 4
F32 = jnp.float32
BF16 = jnp.bfloat16


def place(t):
    return t // 4, (t // 2) % 2, t % 2


def index(z, y, c):
    return z * 4 + y * 2 + c


def in_group(value, dz=0, dy=0, dc=0):
    route = []
    for t in range(4 * NZ):
        z, y, c = place(t)
        route.append((t, index(z ^ dz, y ^ dy, c ^ dc)))
    return lax.ppermute(value, "tensor", route)


def over_all(value, target):
    sections, n_tensor, n_dp = (lax.axis_size(a) for a in ALL)
    route = []
    for s in range(sections):
        for t in range(n_tensor):
            for d in range(n_dp):
                ts, tt, td = target(s, t, d)
                if ts >= 0:
                    here = (s * n_tensor + t) * n_dp + d
                    route.append((here, (ts * n_tensor + tt) * n_dp + td))
    return lax.ppermute(value, ALL, route)


def swap_dp(value):
    return lax.ppermute(value, "dp", [(0, 1), (1, 0)])


def home_parts(value, dp_id, new_section, dy=0):
    own = value.shape[-1] // 2
    left, right = value[..., :own], value[..., own:]
    got = []
    for j in range(2):
        chosen = jnp.where(dp_id == j, left, right)

        def target(s, t, d, j=j):
            b = 2 * t + (j ^ d)
            return new_section(s), (b % 16) ^ (dy << 1), b // 16

        got.append(over_all(chosen, target))
    return got


def to_home(value, dp_id, t_id, new_section, dy=0):
    got = home_parts(value, dp_id, new_section, dy)
    even = t_id % 2 == 0
    return jnp.stack([jnp.where(even, got[0], got[1]), jnp.where(even, got[1], got[0])])


def from_home(value, dp_id, t_id, new_section):
    even = t_id % 2 == 0
    got = []
    for j in range(2):
        chosen = jnp.where(even, value[j], value[1 - j])

        def target(s, t, d, j=j):
            return new_section(s), (16 * d + t) // 2, j ^ (t % 2)

        got.append(over_all(chosen, target))
    first = dp_id == 0
    return jnp.concatenate(
        [jnp.where(first, got[0], got[1]), jnp.where(first, got[1], got[0])], axis=-1
    )


def call(kernel, arrays, specs, gates, mib=3, **settings):
    n = len(arrays)
    settings["compiler_params"] = pltpu.CompilerParams(vmem_limit_bytes=mib * 2**20)

    def body(*refs):
        kernel(*refs[:n], *refs[n + len(gates) :])

    specs = list(specs) + [pl.BlockSpec(memory_space=pl.ANY)] * len(gates)
    return pl.pallas_call(body, in_specs=specs, **settings)(*arrays, *gates)


VMEM = pl.BlockSpec(memory_space=pltpu.VMEM)
SMEM = pl.BlockSpec(memory_space=pltpu.SMEM)
ANY = pl.BlockSpec(memory_space=pl.ANY)


def cost(flops, bytes_accessed):
    return pl.CostEstimate(flops=flops, bytes_accessed=bytes_accessed, transcendentals=0)


def in_vmem(*arrays):
    return [pltpu.with_memory_space_constraint(a, pltpu.VMEM) for a in arrays]


def in_hbm(*arrays):
    return [pltpu.with_memory_space_constraint(a, pltpu.HBM) for a in arrays]


def given_kernel(core, u_ref, w_ref, u_out, w_out, sems):
    block = u_out.shape[0] // 8
    copies = []
    for ref, out in ((u_ref, u_out), (w_ref, w_out)):
        for i in range(8):
            start = pl.multiple_of((2 * i + 1 - core[0]) * block, block)
            copies.append(
                pltpu.make_async_copy(
                    ref.at[pl.ds(start, block)],
                    out.at[pl.ds(i * block, block)],
                    sems.at[len(copies)],
                )
            )
    for copy in copies:
        copy.start()
    for copy in copies:
        copy.wait()


def given(first, second, core):
    rows, cols = first.shape
    return call(
        given_kernel,
        [core, *in_hbm(first, second)],
        [SMEM, ANY, ANY],
        (),
        out_specs=[VMEM] * 2,
        out_shape=[pltpu.VMEM((rows // 2, cols), BF16)] * 2,
        scratch_shapes=[pltpu.SemaphoreType.DMA((16,))],
        mib=8,
        cost_estimate=cost(0, 4 * rows * cols),
    )


def sum_kernel(y, p_ref, a_ref, b_ref, c_ref, g_ref, o_ref):
    own = o_ref.shape[1] // 2
    total = p_ref[...].astype(F32) + a_ref[...].astype(F32)
    total += b_ref[...].astype(F32) + c_ref[...].astype(F32)
    mine = lax.broadcasted_iota(jnp.int32, total.shape, 1) // own == y[0]
    o_ref[...] = (total + jnp.where(mine, g_ref[...].astype(F32), 0)).astype(BF16)


def z_sum(piece, arrived, grad, y, gates):
    return call(
        sum_kernel,
        [y, *in_vmem(piece, *arrived, grad)],
        [SMEM] + [VMEM] * 5,
        gates,
        out_specs=VMEM,
        out_shape=pltpu.VMEM(piece.shape, BF16),
        cost_estimate=cost(6 * piece.size, 12 * piece.size),
    )


def enter_kernel(at, s_ref, a_ref, t_ref, o_ref, own_ref):
    own = own_ref.shape[1]
    total = (s_ref[...].astype(F32) + a_ref[...].astype(F32)).astype(BF16)
    own_ref[...] = jnp.where(at[0] == 0, total[:, :own], total[:, own:])
    o_ref[...] = jnp.where(at[1] == 1, t_ref[...], total)


def enter(straight, across, top, at, gates):
    rows, width = straight.shape
    return call(
        enter_kernel,
        [at, *in_vmem(straight, across, top)],
        [SMEM] + [VMEM] * 3,
        gates,
        out_specs=[VMEM] * 2,
        out_shape=[
            pltpu.VMEM((rows, width), BF16),
            pltpu.VMEM((rows, width // 2), BF16),
        ],
        cost_estimate=cost(2 * straight.size, 8 * straight.size),
    )


def outer_kernel(order, n0, n1, f0, f1, h_ref, o_ref, held, sems):
    own = n0.shape[1] // 8
    heads = h_ref[...]
    copies = []
    for i in range(16):
        at = slice(i % 8 * own, (i % 8 + 1) * own)
        block = [half[:, at] for half in ((n0, n1) if i < 8 else (f0, f1))]
        held[i] = lax.dot_general(
            jnp.concatenate(block, axis=0),
            heads,
            (((0,), (0,)), ((), ())),
            preferred_element_type=F32,
        ).astype(held.dtype)
        start = pl.multiple_of(order[i] * own, own)
        copy = pltpu.make_async_copy(held.at[i], o_ref.at[pl.ds(start, own)], sems.at[i])
        copy.start()
        copies.append(copy)
    for copy in copies:
        copy.wait()


def outer(near, far, heads, order):
    tokens, cols = heads.shape
    width = near[0].shape[1]
    own = width // 8
    return call(
        outer_kernel,
        [order, *near, *far, heads],
        [SMEM] + [VMEM] * 5,
        (),
        out_specs=ANY,
        out_shape=jax.ShapeDtypeStruct((2 * width, cols), BF16),
        scratch_shapes=[pltpu.VMEM((16, own, cols), BF16), pltpu.SemaphoreType.DMA((16,))],
        mib=10,
        cost_estimate=cost(4 * tokens * width * cols, 4 * (tokens * width + width * cols)),
    )


def slots_kernel(slots, held_ref, o_ref, sems):
    copies = [
        pltpu.make_async_copy(held_ref.at[slots[m]], o_ref.at[m], sems.at[m])
        for m in range(o_ref.shape[0])
    ]
    for copy in copies:
        copy.start()
    for copy in copies:
        copy.wait()


def in_slots(held, slots, gates):
    return call(
        slots_kernel,
        [slots, held],
        [SMEM, ANY],
        gates,
        out_specs=VMEM,
        out_shape=pltpu.VMEM(held.shape, BF16),
        scratch_shapes=[pltpu.SemaphoreType.DMA((held.shape[0],))],
        cost_estimate=cost(0, 4 * held.size),
    )


def stash_kernel(odd, a_ref, b_ref, o_ref):
    even = odd[0] == 0
    micro, seq, _ = a_ref.shape
    for m in range(micro):
        for r, (first, second) in enumerate(((a_ref, b_ref), (b_ref, a_ref))):
            at = slice((2 * m + r) * seq, (2 * m + r + 1) * seq)
            o_ref[at, :] = jnp.where(even, first[m], second[m])


def stash_rows(parts, odd, gates):
    micro, seq, own = parts[0].shape
    return call(
        stash_kernel,
        [odd, *parts],
        [SMEM] + [VMEM] * 2,
        gates,
        out_specs=VMEM,
        out_shape=jax.ShapeDtypeStruct((2 * micro * seq, own), BF16),
        cost_estimate=cost(0, 8 * parts[0].size),
    )


def tie_kernel(x_ref, o_ref):
    pass


def tie(value, *gates):
    return call(
        tie_kernel,
        [value],
        [ANY],
        gates,
        out_specs=ANY,
        out_shape=jax.ShapeDtypeStruct(value.shape, value.dtype),
        input_output_aliases={0: 0},
        cost_estimate=cost(0, 0),
    )


def probs_kernel(qk_ref, o_ref):
    micro, n_heads, seq, _ = o_ref.shape
    query = lax.broadcasted_iota(jnp.int32, (seq, seq), 0)
    key = lax.broadcasted_iota(jnp.int32, (seq, seq), 1)
    for m in range(micro):
        for h in range(n_heads):
            at = slice(h * DH, (h + 1) * DH)
            scores = lax.dot_general(
                qk_ref[m, 0, :, at],
                qk_ref[m, 1, :, at],
                (((1,), (1,)), ((), ())),
                preferred_element_type=F32,
            )
            scores = jnp.where(key <= query, scores * DH ** (-0.5), -jnp.inf)
            weights = jnp.exp(scores - jnp.max(scores, axis=-1, keepdims=True))
            weights = weights / jnp.sum(weights, axis=-1, keepdims=True)
            o_ref[m, h] = weights.astype(o_ref.dtype)


def attention_probs(query_key, gates):
    micro, _, seq, cols = query_key.shape
    return call(
        probs_kernel,
        [query_key],
        [VMEM],
        gates,
        out_specs=VMEM,
        out_shape=jax.ShapeDtypeStruct((micro, cols // DH, seq, seq), BF16),
        cost_estimate=cost(2 * micro * seq * seq * cols, 2 * query_key.size),
    )


def heads_kernel(turned, n_micro, position, mine_ref, there_ref, probs_ref, o_ref):
    total = (mine_ref[...].astype(F32) + there_ref[...].astype(F32)).astype(BF16)
    _, n_rep, n_heads, seq, _ = probs_ref.shape
    for m in range(n_micro):
        for r in range(n_rep):
            for h in range(n_heads):
                rows = slice((m * n_rep + r) * seq, (m * n_rep + r + 1) * seq)
                cols = slice(h * DH, (h + 1) * DH)
                o_ref[rows, cols] = lax.dot_general(
                    probs_ref[position[0] + m, r, h],
                    total[rows, cols],
                    (((0 if turned else 1,), (0,)), ((), ())),
                    preferred_element_type=F32,
                ).astype(o_ref.dtype)


def head_products(mine, there, probs, position, turned, gates):
    n_micro = mine.shape[0] // (probs.shape[1] * probs.shape[3])
    return call(
        functools.partial(heads_kernel, turned, n_micro),
        [position, *in_vmem(mine, there, probs)],
        [SMEM] + [VMEM] * 3,
        gates,
        out_specs=VMEM,
        out_shape=pltpu.VMEM(mine.shape, BF16),
        cost_estimate=cost(2 * mine.size * probs.shape[-1], 6 * mine.size),
    )


def weight_copies(order, own_ref, got_ref, held, sems):
    block = held.shape[1] // 2
    copies = []
    for k in range(NZ):
        group = []
        for y in range(2):
            t = order[2 * k + y]
            at = pl.ds(y * block, block)
            cols = own_ref.shape[1]
            own = own_ref.at[pl.ds(pl.multiple_of(t * block, block), block)]
            got = got_ref.at[pl.ds(pl.multiple_of(t // 2 * block, block), block)]
            sem = sems.at[2 * (2 * k + y)], sems.at[2 * (2 * k + y) + 1]
            group.append(pltpu.make_async_copy(own, held.at[k, at, pl.ds(0, cols)], sem[0]))
            group.append(pltpu.make_async_copy(got, held.at[k, at, pl.ds(cols, cols)], sem[1]))
        copies.append(group)
    return copies


def load_kernel(turned, order, own_ref, got_ref, o_ref, *scratch):
    held = scratch[0] if turned else o_ref
    copies = weight_copies(order, own_ref, got_ref, held, scratch[-1])
    for group in copies:
        for copy in group:
            copy.start()
    for k, group in enumerate(copies):
        for copy in group:
            copy.wait()
        if turned:
            o_ref[k] = held[k].T


def load(own, got, order, turned, gates):
    width, cols = own.shape[0] // (2 * NZ), 2 * own.shape[1]
    held = [pltpu.VMEM((NZ, width, cols), BF16)] if turned else []
    shape = (NZ, cols, width) if turned else (NZ, width, cols)
    return call(
        functools.partial(load_kernel, turned),
        [order, *in_hbm(own, got)],
        [SMEM, ANY, ANY],
        gates,
        out_specs=VMEM,
        out_shape=pltpu.VMEM(shape, BF16),
        scratch_shapes=held + [pltpu.SemaphoreType.DMA((4 * NZ,))],
        mib=11 if turned else 6,
        cost_estimate=cost(0, 8 * NZ * width * cols),
    )


def gather_kernel(a0, a1, a2, a3, w_ref, keep_ref, give_ref, total):
    cols = keep_ref.shape[1]
    for k, a in enumerate((a0, a1, a2, a3)):
        term = jnp.dot(a[...], w_ref[k], preferred_element_type=F32)
        if k == 0:
            total[...] = term
        elif k < NZ - 1:
            total[...] += term
        else:
            term = term + total[...]
            keep_ref[...] = term[:, :cols]
            give_ref[...] = term[:, cols:].astype(give_ref.dtype)


def gather_product(pieces, weights, gates):
    rows, width = pieces[0].shape
    cols = weights.shape[2] // 2
    return call(
        gather_kernel,
        in_vmem(*pieces, weights),
        [VMEM] * 5,
        gates,
        out_specs=[VMEM] * 2,
        out_shape=[pltpu.VMEM((rows, cols), F32), pltpu.VMEM((rows, cols), BF16)],
        scratch_shapes=[pltpu.VMEM((rows, 2 * cols), F32)],
        mib=3,
        cost_estimate=cost(16 * rows * width * cols, 16 * width * cols),
    )


def branch_kernel(v_ref, c_ref, w_ref, o0, o1, o2, o3):
    both = jnp.concatenate([v_ref[...], c_ref[...]], axis=1)
    for k, out in enumerate((o0, o1, o2, o3)):
        out[...] = jnp.dot(both, w_ref[k], preferred_element_type=F32).astype(BF16)


def branch_product(vals, vals_core, weights):
    rows, cols = vals.shape
    width = weights.shape[2]
    return call(
        branch_kernel,
        in_vmem(vals, vals_core, weights),
        [VMEM] * 3,
        (),
        out_specs=[VMEM] * 4,
        out_shape=[pltpu.VMEM((rows, width), BF16)] * 4,
        mib=3,
        cost_estimate=cost(16 * rows * width * cols, 16 * width * cols),
    )


def pick_kernel(section, *refs):
    grads, near_ref, sems = refs[:-2], *refs[-2:]
    n = sems.shape[0]
    sections = len(grads) // n
    width = grads[0].shape[1]
    for s in range(sections):

        @pl.when(section[0] == s)
        def _(s=s):
            copies = []
            for k in range(n):
                copies.append(
                    pltpu.make_async_copy(
                        grads[s * n + k], near_ref.at[:, pl.ds(k * width, width)], sems.at[k]
                    )
                )
            for copy in copies:
                copy.start()
            for copy in copies:
                copy.wait()


def pick(grads, section, gates, n=NZ, fresh=0):
    rows, width = grads[0][0].shape
    flat = [piece for entry in grads for piece in entry]
    flat = in_vmem(*flat[: fresh * n]) + in_hbm(*flat[fresh * n :])
    return call(
        pick_kernel,
        [section, *flat],
        [SMEM] + [VMEM] * (fresh * n) + [ANY] * (len(flat) - fresh * n),
        gates,
        out_specs=VMEM,
        out_shape=pltpu.VMEM((rows, n * width), BF16),
        scratch_shapes=[pltpu.SemaphoreType.DMA((n,))],
        cost_estimate=cost(0, 4 * rows * n * width),
    )


def pick_one(seen, section, gates, fresh=0):
    return pick([[one] for one in seen], section, gates, 1, fresh)


def dot(a, b):
    return jnp.dot(a, b, preferred_element_type=F32)


def on_device(held_input, query_key, w_value, w_out, grad_top, slot_table):
    sections = lax.axis_size("section")
    section_id = lax.axis_index("section")
    t_id = lax.axis_index("tensor")
    dp_id = lax.axis_index("dp")
    z, y, c = place(t_id)
    micro, seq, two_own = held_input.shape[2:]
    own = two_own // 2
    local_cols = w_value.shape[2]
    heads = local_cols // DH
    rows = 2 * seq
    lower = y == 0

    same, other = (to_home(grad_top[0], dp_id, t_id, lambda s: s, dy) for dy in range(2))
    pair = [jnp.where(lower, same, other), jnp.where(lower, other, same)]
    tops = jnp.swapaxes(jnp.concatenate(pair, axis=-1), 0, 1).reshape(micro, rows, two_own)
    top = tops[0]

    order = [index(z ^ k, yy, c) for k in range(NZ) for yy in range(2)]
    order = jnp.stack(order + [t ^ 1 for t in order]).astype(jnp.int32)

    core = c.astype(jnp.int32).reshape(1)
    section = section_id.astype(jnp.int32).reshape(1)
    at = jnp.stack([y, section_id == sections - 1]).astype(jnp.int32)

    out_given, value_given = given(w_out[0], w_value[0], core)
    out_got = in_group(out_given, dc=1)
    value_got = in_group(value_given, dc=1)

    probs = attention_probs(query_key[0, 0], (out_got,))
    probs_there = swap_dp(probs)
    first = dp_id == 0
    probs = jnp.stack(
        [jnp.where(first, probs, probs_there), jnp.where(first, probs_there, probs)], axis=1
    )

    tick_total = micro + sections - 1
    incoming = top
    out_ready = load(w_out[0], out_got, order, False, ())
    grads_seen, values_seen, inputs_seen = [], [], []
    stash = values = values_there = heads_out = layer_in = None

    def chosen(seen):
        return lax.select_n(section_id, *seen)

    for tick in range(tick_total):
        last = tick == tick_total - 1
        position = jnp.clip(tick - (sections - 1 - section_id), 0, micro - 1)
        position = position.astype(jnp.int32).reshape(1)
        near = [incoming] + [in_group(incoming, dz=k) for k in range(1, NZ)]
        grads_seen.append(near)
        gates = ()
        if tick == 1:
            stash = stash_rows(stash, c.astype(jnp.int32).reshape(1), (incoming,))
            layer_in = lax.all_gather(stash, "tensor", axis=1, tiled=True)
        if last:
            first_grads = pick(grads_seen[:sections][::-1], section, (incoming,))
            ends = [
                pick_one(
                    [
                        inputs_seen[min(sections - 1 - (s + 1) % sections + m, tick - 1)]
                        for s in range(sections)
                    ],
                    section,
                    (incoming,),
                )
                for m in range(micro)
            ]
            early = from_home(
                jnp.stack([end.reshape(2, seq, own) for end in ends], axis=1),
                dp_id,
                t_id,
                lambda s: (s + 1) % sections,
            )
            first_values = pick_one(values_seen[::-1], section, (incoming,))
            gates = (first_grads, first_values, *ends)
        keep, give = gather_product(near, out_ready, gates)
        from_core = in_group(give, dc=1)
        grad_heads = (keep + from_core.astype(F32)).astype(BF16)
        there = swap_dp(grad_heads)
        value_ready = load(w_value[0], value_got, order, True, (grad_heads,))
        gates = (value_ready,)
        if tick == 3:
            heads_out = head_products(
                values, values_there, probs, jnp.zeros((1,), jnp.int32), False, (grad_heads,)
            )
            gates += (heads_out,)
        if last:
            later_grads = pick(grads_seen[1:][::-1], section, (grad_heads,), fresh=1)
            gates += (later_grads,)
        grad_vals = head_products(grad_heads, there, probs, position, True, gates)
        values_seen.append(grad_vals)
        pieces = branch_product(grad_vals, in_group(grad_vals, dc=1), value_ready)
        arrived = [in_group(pieces[k], dz=k) for k in range(1, NZ)]
        gates = ()
        if last:
            far = [
                in_group(tie(picked, pieces[0]), dc=1) for picked in (first_grads, later_grads)
            ]
            grad_w_out = outer([first_grads, later_grads], far, heads_out, order)
            later_values = pick_one(values_seen[1:][::-1], section, (pieces[0],), 1)
            grad_w_value = lax.dot_general(
                layer_in,
                jnp.concatenate([first_values, later_values], axis=0),
                (((0,), (0,)), ((), ())),
                preferred_element_type=F32,
            ).astype(BF16)
            gates = (grad_w_value, *in_hbm(grad_w_out))
        sent = z_sum(pieces[0], arrived, incoming, at[:1], gates)
        if tick == 0:
            slot_row = lax.dynamic_index_in_dim(
                slot_table, sections - 1 - section_id, 0, keepdims=False
            )
            ordered = in_slots(held_input[0, 0], slot_row, (sent,))
            stash = home_parts(ordered, dp_id, lambda s: sections - 1 - s)
        if last:
            across = in_group(sent, dy=1)
            _, done = enter(sent, across, sent, at, ())
        else:
            straight = over_all(sent, lambda s, t, d: ((s - 1) % sections, t, d))
            across = over_all(sent, lambda s, t, d: ((s - 1) % sections, t ^ 2, d))
            out_ready = load(w_out[0], out_got, order, False, (sent,))
            gates = ()
            if tick == 2:
                values = dot(layer_in, w_value[0]).astype(BF16)
                values_there = swap_dp(values)
                gates = (values,)
            incoming, completed = enter(straight, across, tops[1], at, gates)
            inputs_seen.append(completed)

    late = from_home(done.reshape(2, seq, own), dp_id, t_id, lambda s: s if s == 0 else -1)
    late = jnp.where(section_id == 0, late, early[micro - 1])
    grad_input = jnp.stack([*early[: micro - 1], late])
    return grad_input[None, None], grad_w_value[None], grad_w_out[None]


def solution(mesh):
    return jax.shard_map(
        on_device,
        mesh=mesh,
        in_specs=(
            P("section", "dp", None, None, "tensor"),
            P("section", "dp", None, None, None, "tensor"),
            P("section", "dp", "tensor"),
            P("section", "dp", "tensor"),
            P("dp", None, None, "tensor"),
            P(),
        ),
        out_specs=(
            P("section", "dp", None, None, "tensor"),
            P("section", "dp", "tensor"),
            P("section", "dp", "tensor"),
        ),
        check_vma=False,
    )
```

```python
import functools

import jax
import jax.numpy as jnp
from jax import lax
from jax.experimental import pallas as pl
from jax.experimental.pallas import tpu as pltpu
from jax.sharding import PartitionSpec as P

DH = 128
ALL = ("section", "tensor", "dp")
NZ = 4
F32 = jnp.float32
BF16 = jnp.bfloat16


def place(t):
    return t // 4, (t // 2) % 2, t % 2


def index(z, y, c):
    return z * 4 + y * 2 + c


def in_group(value, dz=0, dy=0, dc=0):
    route = []
    for t in range(4 * NZ):
        z, y, c = place(t)
        route.append((t, index(z ^ dz, y ^ dy, c ^ dc)))
    return lax.ppermute(value, "tensor", route)


def over_all(value, target):
    sections, n_tensor, n_dp = (lax.axis_size(a) for a in ALL)
    route = []
    for s in range(sections):
        for t in range(n_tensor):
            for d in range(n_dp):
                ts, tt, td = target(s, t, d)
                if ts >= 0:
                    here = (s * n_tensor + t) * n_dp + d
                    route.append((here, (ts * n_tensor + tt) * n_dp + td))
    return lax.ppermute(value, ALL, route)


def swap_dp(value):
    return lax.ppermute(value, "dp", [(0, 1), (1, 0)])


def home_parts(value, dp_id, new_section, dy=0):
    own = value.shape[-1] // 2
    left, right = value[..., :own], value[..., own:]
    got = []
    for j in range(2):
        chosen = jnp.where(dp_id == j, left, right)

        def target(s, t, d, j=j):
            b = 2 * t + (j ^ d)
            return new_section(s), (b % 16) ^ (dy << 1), b // 16

        got.append(over_all(chosen, target))
    return got


def to_home(value, dp_id, t_id, new_section, dy=0):
    got = home_parts(value, dp_id, new_section, dy)
    even = t_id % 2 == 0
    return jnp.stack([jnp.where(even, got[0], got[1]), jnp.where(even, got[1], got[0])])


def from_home(value, dp_id, t_id, new_section):
    even = t_id % 2 == 0
    got = []
    for j in range(2):
        chosen = jnp.where(even, value[j], value[1 - j])

        def target(s, t, d, j=j):
            return new_section(s), (16 * d + t) // 2, j ^ (t % 2)

        got.append(over_all(chosen, target))
    first = dp_id == 0
    return jnp.concatenate(
        [jnp.where(first, got[0], got[1]), jnp.where(first, got[1], got[0])], axis=-1
    )


def call(kernel, arrays, specs, gates, mib=3, **settings):
    n = len(arrays)
    settings["compiler_params"] = pltpu.CompilerParams(vmem_limit_bytes=mib * 2**20)

    def body(*refs):
        kernel(*refs[:n], *refs[n + len(gates) :])

    specs = list(specs) + [pl.BlockSpec(memory_space=pl.ANY)] * len(gates)
    return pl.pallas_call(body, in_specs=specs, **settings)(*arrays, *gates)


VMEM = pl.BlockSpec(memory_space=pltpu.VMEM)
SMEM = pl.BlockSpec(memory_space=pltpu.SMEM)
ANY = pl.BlockSpec(memory_space=pl.ANY)


def cost(flops, bytes_accessed):
    return pl.CostEstimate(flops=flops, bytes_accessed=bytes_accessed, transcendentals=0)


def in_vmem(*arrays):
    return [pltpu.with_memory_space_constraint(a, pltpu.VMEM) for a in arrays]


def in_hbm(*arrays):
    return [pltpu.with_memory_space_constraint(a, pltpu.HBM) for a in arrays]


def given_kernel(core, u_ref, w_ref, u_out, w_out, sems):
    block = u_out.shape[0] // 8
    copies = []
    for ref, out in ((u_ref, u_out), (w_ref, w_out)):
        for i in range(8):
            start = pl.multiple_of((2 * i + 1 - core[0]) * block, block)
            copies.append(
                pltpu.make_async_copy(
                    ref.at[pl.ds(start, block)],
                    out.at[pl.ds(i * block, block)],
                    sems.at[len(copies)],
                )
            )
    for copy in copies:
        copy.start()
    for copy in copies:
        copy.wait()


def given(first, second, core):
    rows, cols = first.shape
    return call(
        given_kernel,
        [core, *in_hbm(first, second)],
        [SMEM, ANY, ANY],
        (),
        out_specs=[VMEM] * 2,
        out_shape=[pltpu.VMEM((rows // 2, cols), BF16)] * 2,
        scratch_shapes=[pltpu.SemaphoreType.DMA((16,))],
        mib=8,
        cost_estimate=cost(0, 4 * rows * cols),
    )


def sum_kernel(y, p_ref, a_ref, b_ref, c_ref, g_ref, o_ref):
    own = o_ref.shape[1] // 2
    total = p_ref[...].astype(F32) + a_ref[...].astype(F32)
    total += b_ref[...].astype(F32) + c_ref[...].astype(F32)
    mine = lax.broadcasted_iota(jnp.int32, total.shape, 1) // own == y[0]
    o_ref[...] = (total + jnp.where(mine, g_ref[...].astype(F32), 0)).astype(BF16)


def z_sum(piece, arrived, grad, y, gates):
    return call(
        sum_kernel,
        [y, *in_vmem(piece, *arrived, grad)],
        [SMEM] + [VMEM] * 5,
        gates,
        out_specs=VMEM,
        out_shape=pltpu.VMEM(piece.shape, BF16),
        cost_estimate=cost(6 * piece.size, 12 * piece.size),
    )


def enter_kernel(at, s_ref, a_ref, t_ref, o_ref, own_ref):
    own = own_ref.shape[1]
    total = (s_ref[...].astype(F32) + a_ref[...].astype(F32)).astype(BF16)
    own_ref[...] = jnp.where(at[0] == 0, total[:, :own], total[:, own:])
    o_ref[...] = jnp.where(at[1] == 1, t_ref[...], total)


def enter(straight, across, top, at, gates):
    rows, width = straight.shape
    return call(
        enter_kernel,
        [at, *in_vmem(straight, across, top)],
        [SMEM] + [VMEM] * 3,
        gates,
        out_specs=[VMEM] * 2,
        out_shape=[
            pltpu.VMEM((rows, width), BF16),
            pltpu.VMEM((rows, width // 2), BF16),
        ],
        cost_estimate=cost(2 * straight.size, 8 * straight.size),
    )


def outer_kernel(order, n0, n1, f0, f1, h_ref, o_ref, held, sems):
    own = n0.shape[1] // 8
    heads = h_ref[...]
    copies = []
    for i in range(16):
        at = slice(i % 8 * own, (i % 8 + 1) * own)
        block = [half[:, at] for half in ((n0, n1) if i < 8 else (f0, f1))]
        held[i] = lax.dot_general(
            jnp.concatenate(block, axis=0),
            heads,
            (((0,), (0,)), ((), ())),
            preferred_element_type=F32,
        ).astype(held.dtype)
        start = pl.multiple_of(order[i] * own, own)
        copy = pltpu.make_async_copy(held.at[i], o_ref.at[pl.ds(start, own)], sems.at[i])
        copy.start()
        copies.append(copy)
    for copy in copies:
        copy.wait()


def outer(near, far, heads, order):
    tokens, cols = heads.shape
    width = near[0].shape[1]
    own = width // 8
    return call(
        outer_kernel,
        [order, *near, *far, heads],
        [SMEM] + [VMEM] * 5,
        (),
        out_specs=ANY,
        out_shape=jax.ShapeDtypeStruct((2 * width, cols), BF16),
        scratch_shapes=[pltpu.VMEM((16, own, cols), BF16), pltpu.SemaphoreType.DMA((16,))],
        mib=10,
        cost_estimate=cost(4 * tokens * width * cols, 4 * (tokens * width + width * cols)),
    )


def slots_kernel(slots, held_ref, o_ref, sems):
    copies = [
        pltpu.make_async_copy(held_ref.at[slots[m]], o_ref.at[m], sems.at[m])
        for m in range(o_ref.shape[0])
    ]
    for copy in copies:
        copy.start()
    for copy in copies:
        copy.wait()


def in_slots(held, slots, gates):
    return call(
        slots_kernel,
        [slots, held],
        [SMEM, ANY],
        gates,
        out_specs=VMEM,
        out_shape=pltpu.VMEM(held.shape, BF16),
        scratch_shapes=[pltpu.SemaphoreType.DMA((held.shape[0],))],
        cost_estimate=cost(0, 4 * held.size),
    )


def stash_kernel(odd, a_ref, b_ref, o_ref):
    even = odd[0] == 0
    micro, seq, _ = a_ref.shape
    for m in range(micro):
        for r, (first, second) in enumerate(((a_ref, b_ref), (b_ref, a_ref))):
            at = slice((2 * m + r) * seq, (2 * m + r + 1) * seq)
            o_ref[at, :] = jnp.where(even, first[m], second[m])


def stash_rows(parts, odd, gates):
    micro, seq, own = parts[0].shape
    return call(
        stash_kernel,
        [odd, *parts],
        [SMEM] + [VMEM] * 2,
        gates,
        out_specs=VMEM,
        out_shape=jax.ShapeDtypeStruct((2 * micro * seq, own), BF16),
        cost_estimate=cost(0, 8 * parts[0].size),
    )


def tie_kernel(x_ref, o_ref):
    pass


def tie(value, *gates):
    return call(
        tie_kernel,
        [value],
        [ANY],
        gates,
        out_specs=ANY,
        out_shape=jax.ShapeDtypeStruct(value.shape, value.dtype),
        input_output_aliases={0: 0},
        cost_estimate=cost(0, 0),
    )


def probs_kernel(qk_ref, o_ref):
    micro, n_heads, seq, _ = o_ref.shape
    query = lax.broadcasted_iota(jnp.int32, (seq, seq), 0)
    key = lax.broadcasted_iota(jnp.int32, (seq, seq), 1)
    for m in range(micro):
        for h in range(n_heads):
            at = slice(h * DH, (h + 1) * DH)
            scores = lax.dot_general(
                qk_ref[m, 0, :, at],
                qk_ref[m, 1, :, at],
                (((1,), (1,)), ((), ())),
                preferred_element_type=F32,
            )
            scores = jnp.where(key <= query, scores * DH ** (-0.5), -jnp.inf)
            weights = jnp.exp(scores - jnp.max(scores, axis=-1, keepdims=True))
            weights = weights / jnp.sum(weights, axis=-1, keepdims=True)
            o_ref[m, h] = weights.astype(o_ref.dtype)


def attention_probs(query_key, gates):
    micro, _, seq, cols = query_key.shape
    return call(
        probs_kernel,
        [query_key],
        [VMEM],
        gates,
        out_specs=VMEM,
        out_shape=jax.ShapeDtypeStruct((micro, cols // DH, seq, seq), BF16),
        cost_estimate=cost(2 * micro * seq * seq * cols, 2 * query_key.size),
    )


def heads_kernel(turned, n_micro, position, mine_ref, there_ref, probs_ref, o_ref):
    total = (mine_ref[...].astype(F32) + there_ref[...].astype(F32)).astype(BF16)
    _, n_rep, n_heads, seq, _ = probs_ref.shape
    for m in range(n_micro):
        for r in range(n_rep):
            for h in range(n_heads):
                rows = slice((m * n_rep + r) * seq, (m * n_rep + r + 1) * seq)
                cols = slice(h * DH, (h + 1) * DH)
                o_ref[rows, cols] = lax.dot_general(
                    probs_ref[position[0] + m, r, h],
                    total[rows, cols],
                    (((0 if turned else 1,), (0,)), ((), ())),
                    preferred_element_type=F32,
                ).astype(o_ref.dtype)


def head_products(mine, there, probs, position, turned, gates):
    n_micro = mine.shape[0] // (probs.shape[1] * probs.shape[3])
    return call(
        functools.partial(heads_kernel, turned, n_micro),
        [position, *in_vmem(mine, there, probs)],
        [SMEM] + [VMEM] * 3,
        gates,
        out_specs=VMEM,
        out_shape=pltpu.VMEM(mine.shape, BF16),
        cost_estimate=cost(2 * mine.size * probs.shape[-1], 6 * mine.size),
    )


def weight_copies(order, own_ref, got_ref, held, sems):
    block = held.shape[1] // 2
    copies = []
    for k in range(NZ):
        group = []
        for y in range(2):
            t = order[2 * k + y]
            at = pl.ds(y * block, block)
            cols = own_ref.shape[1]
            own = own_ref.at[pl.ds(pl.multiple_of(t * block, block), block)]
            got = got_ref.at[pl.ds(pl.multiple_of(t // 2 * block, block), block)]
            sem = sems.at[2 * (2 * k + y)], sems.at[2 * (2 * k + y) + 1]
            group.append(pltpu.make_async_copy(own, held.at[k, at, pl.ds(0, cols)], sem[0]))
            group.append(pltpu.make_async_copy(got, held.at[k, at, pl.ds(cols, cols)], sem[1]))
        copies.append(group)
    return copies


def load_kernel(turned, order, own_ref, got_ref, o_ref, *scratch):
    held = scratch[0] if turned else o_ref
    copies = weight_copies(order, own_ref, got_ref, held, scratch[-1])
    for group in copies:
        for copy in group:
            copy.start()
    for k, group in enumerate(copies):
        for copy in group:
            copy.wait()
        if turned:
            o_ref[k] = held[k].T


def load(own, got, order, turned, gates):
    width, cols = own.shape[0] // (2 * NZ), 2 * own.shape[1]
    held = [pltpu.VMEM((NZ, width, cols), BF16)] if turned else []
    shape = (NZ, cols, width) if turned else (NZ, width, cols)
    return call(
        functools.partial(load_kernel, turned),
        [order, *in_hbm(own, got)],
        [SMEM, ANY, ANY],
        gates,
        out_specs=VMEM,
        out_shape=pltpu.VMEM(shape, BF16),
        scratch_shapes=held + [pltpu.SemaphoreType.DMA((4 * NZ,))],
        mib=11 if turned else 6,
        cost_estimate=cost(0, 8 * NZ * width * cols),
    )


def gather_kernel(a0, a1, a2, a3, w_ref, keep_ref, give_ref, total):
    cols = keep_ref.shape[1]
    for k, a in enumerate((a0, a1, a2, a3)):
        term = jnp.dot(a[...], w_ref[k], preferred_element_type=F32)
        if k == 0:
            total[...] = term
        elif k < NZ - 1:
            total[...] += term
        else:
            term = term + total[...]
            keep_ref[...] = term[:, :cols]
            give_ref[...] = term[:, cols:].astype(give_ref.dtype)


def gather_product(pieces, weights, gates):
    rows, width = pieces[0].shape
    cols = weights.shape[2] // 2
    return call(
        gather_kernel,
        in_vmem(*pieces, weights),
        [VMEM] * 5,
        gates,
        out_specs=[VMEM] * 2,
        out_shape=[pltpu.VMEM((rows, cols), F32), pltpu.VMEM((rows, cols), BF16)],
        scratch_shapes=[pltpu.VMEM((rows, 2 * cols), F32)],
        mib=3,
        cost_estimate=cost(16 * rows * width * cols, 16 * width * cols),
    )


def branch_kernel(v_ref, c_ref, w_ref, o0, o1, o2, o3):
    both = jnp.concatenate([v_ref[...], c_ref[...]], axis=1)
    for k, out in enumerate((o0, o1, o2, o3)):
        out[...] = jnp.dot(both, w_ref[k], preferred_element_type=F32).astype(BF16)


def branch_product(vals, vals_core, weights):
    rows, cols = vals.shape
    width = weights.shape[2]
    return call(
        branch_kernel,
        in_vmem(vals, vals_core, weights),
        [VMEM] * 3,
        (),
        out_specs=[VMEM] * 4,
        out_shape=[pltpu.VMEM((rows, width), BF16)] * 4,
        mib=3,
        cost_estimate=cost(16 * rows * width * cols, 16 * width * cols),
    )


def pick_kernel(section, *refs):
    grads, near_ref, sems = refs[:-2], *refs[-2:]
    n = sems.shape[0]
    sections = len(grads) // n
    width = grads[0].shape[1]
    for s in range(sections):

        @pl.when(section[0] == s)
        def _(s=s):
            copies = []
            for k in range(n):
                copies.append(
                    pltpu.make_async_copy(
                        grads[s * n + k], near_ref.at[:, pl.ds(k * width, width)], sems.at[k]
                    )
                )
            for copy in copies:
                copy.start()
            for copy in copies:
                copy.wait()


def pick(grads, section, gates, n=NZ, fresh=0):
    rows, width = grads[0][0].shape
    flat = [piece for entry in grads for piece in entry]
    flat = in_vmem(*flat[: fresh * n]) + in_hbm(*flat[fresh * n :])
    return call(
        pick_kernel,
        [section, *flat],
        [SMEM] + [VMEM] * (fresh * n) + [ANY] * (len(flat) - fresh * n),
        gates,
        out_specs=VMEM,
        out_shape=pltpu.VMEM((rows, n * width), BF16),
        scratch_shapes=[pltpu.SemaphoreType.DMA((n,))],
        cost_estimate=cost(0, 4 * rows * n * width),
    )


def pick_one(seen, section, gates, fresh=0):
    return pick([[one] for one in seen], section, gates, 1, fresh)


def dot(a, b):
    return jnp.dot(a, b, preferred_element_type=F32)


def on_device(held_input, query_key, w_value, w_out, grad_top, slot_table):
    sections = lax.axis_size("section")
    section_id = lax.axis_index("section")
    t_id = lax.axis_index("tensor")
    dp_id = lax.axis_index("dp")
    z, y, c = place(t_id)
    micro, seq, two_own = held_input.shape[2:]
    own = two_own // 2
    local_cols = w_value.shape[2]
    heads = local_cols // DH
    rows = 2 * seq
    lower = y == 0

    same, other = (to_home(grad_top[0], dp_id, t_id, lambda s: s, dy) for dy in range(2))
    pair = [jnp.where(lower, same, other), jnp.where(lower, other, same)]
    tops = jnp.swapaxes(jnp.concatenate(pair, axis=-1), 0, 1).reshape(micro, rows, two_own)
    top = tops[0]

    order = [index(z ^ k, yy, c) for k in range(NZ) for yy in range(2)]
    order = jnp.stack(order + [t ^ 1 for t in order]).astype(jnp.int32)

    core = c.astype(jnp.int32).reshape(1)
    section = section_id.astype(jnp.int32).reshape(1)
    at = jnp.stack([y, section_id == sections - 1]).astype(jnp.int32)

    out_given, value_given = given(w_out[0], w_value[0], core)
    out_got = in_group(out_given, dc=1)
    value_got = in_group(value_given, dc=1)

    probs = attention_probs(query_key[0, 0], (out_got,))
    probs_there = swap_dp(probs)
    first = dp_id == 0
    probs = jnp.stack(
        [jnp.where(first, probs, probs_there), jnp.where(first, probs_there, probs)], axis=1
    )

    tick_total = micro + sections - 1
    incoming = top
    out_ready = load(w_out[0], out_got, order, False, ())
    grads_seen, values_seen, inputs_seen = [], [], []
    stash = values = values_there = heads_out = layer_in = None

    def chosen(seen):
        return lax.select_n(section_id, *seen)

    for tick in range(tick_total):
        last = tick == tick_total - 1
        position = jnp.clip(tick - (sections - 1 - section_id), 0, micro - 1)
        position = position.astype(jnp.int32).reshape(1)
        near = {k: in_group(incoming, dz=k) for k in (2, 1, 3)}
        near = [incoming] + [near[k] for k in range(1, NZ)]
        grads_seen.append(near)
        gates = ()
        if tick == 1:
            stash = stash_rows(stash, c.astype(jnp.int32).reshape(1), (incoming,))
            layer_in = lax.all_gather(stash, "tensor", axis=1, tiled=True)
        if last:
            first_grads = pick(grads_seen[:sections][::-1], section, (incoming,))
            ends = [
                pick_one(
                    [
                        inputs_seen[min(sections - 1 - (s + 1) % sections + m, tick - 1)]
                        for s in range(sections)
                    ],
                    section,
                    (incoming,),
                )
                for m in range(micro)
            ]
            early = from_home(
                jnp.stack([end.reshape(2, seq, own) for end in ends], axis=1),
                dp_id,
                t_id,
                lambda s: (s + 1) % sections,
            )
            first_values = pick_one(values_seen[::-1], section, (incoming,))
            gates = (first_grads, first_values, *ends)
        keep, give = gather_product(near, out_ready, gates)
        from_core = in_group(give, dc=1)
        grad_heads = (keep + from_core.astype(F32)).astype(BF16)
        there = swap_dp(grad_heads)
        value_ready = load(w_value[0], value_got, order, True, (grad_heads,))
        gates = (value_ready,)
        if tick == 3:
            heads_out = head_products(
                values, values_there, probs, jnp.zeros((1,), jnp.int32), False, (grad_heads,)
            )
            gates += (heads_out,)
        if last:
            later_grads = pick(grads_seen[1:][::-1], section, (grad_heads,), fresh=1)
            gates += (later_grads,)
        grad_vals = head_products(grad_heads, there, probs, position, True, gates)
        values_seen.append(grad_vals)
        pieces = branch_product(grad_vals, in_group(grad_vals, dc=1), value_ready)
        arrived = [in_group(pieces[k], dz=k) for k in (2, 1, 3)]
        gates = ()
        if last:
            far = [
                in_group(tie(picked, pieces[0]), dc=1) for picked in (first_grads, later_grads)
            ]
            grad_w_out = outer([first_grads, later_grads], far, heads_out, order)
            later_values = pick_one(values_seen[1:][::-1], section, (pieces[0],), 1)
            grad_w_value = lax.dot_general(
                layer_in,
                jnp.concatenate([first_values, later_values], axis=0),
                (((0,), (0,)), ((), ())),
                preferred_element_type=F32,
            ).astype(BF16)
            gates = (grad_w_value, *in_hbm(grad_w_out))
        sent = z_sum(pieces[0], arrived, incoming, at[:1], gates)
        if tick == 0:
            slot_row = lax.dynamic_index_in_dim(
                slot_table, sections - 1 - section_id, 0, keepdims=False
            )
            ordered = in_slots(held_input[0, 0], slot_row, (sent,))
            stash = home_parts(ordered, dp_id, lambda s: sections - 1 - s)
        if last:
            across = in_group(sent, dy=1)
            _, done = enter(sent, across, sent, at, ())
        else:
            straight = over_all(sent, lambda s, t, d: ((s - 1) % sections, t, d))
            across = over_all(sent, lambda s, t, d: ((s - 1) % sections, t ^ 2, d))
            out_ready = load(w_out[0], out_got, order, False, (sent,))
            gates = ()
            if tick == 2:
                values = dot(layer_in, w_value[0]).astype(BF16)
                values_there = swap_dp(values)
                gates = (values,)
            incoming, completed = enter(straight, across, tops[1], at, gates)
            inputs_seen.append(completed)

    late = from_home(done.reshape(2, seq, own), dp_id, t_id, lambda s: s if s == 0 else -1)
    late = jnp.where(section_id == 0, late, early[micro - 1])
    grad_input = jnp.stack([*early[: micro - 1], late])
    return grad_input[None, None], grad_w_value[None], grad_w_out[None]


def solution(mesh):
    return jax.shard_map(
        on_device,
        mesh=mesh,
        in_specs=(
            P("section", "dp", None, None, "tensor"),
            P("section", "dp", None, None, None, "tensor"),
            P("section", "dp", "tensor"),
            P("section", "dp", "tensor"),
            P("dp", None, None, "tensor"),
            P(),
        ),
        out_specs=(
            P("section", "dp", None, None, "tensor"),
            P("section", "dp", "tensor"),
            P("section", "dp", "tensor"),
        ),
        check_vma=False,
    )
```

```python
import functools

import jax
import jax.numpy as jnp
from jax import lax
from jax.experimental import pallas as pl
from jax.experimental.pallas import tpu as pltpu
from jax.sharding import PartitionSpec as P

DH = 128
ALL = ("section", "tensor", "dp")
NZ = 4
F32 = jnp.float32
BF16 = jnp.bfloat16


def place(t):
    return t // 4, (t // 2) % 2, t % 2


def index(z, y, c):
    return z * 4 + y * 2 + c


def in_group(value, dz=0, dy=0, dc=0):
    route = []
    for t in range(4 * NZ):
        z, y, c = place(t)
        route.append((t, index(z ^ dz, y ^ dy, c ^ dc)))
    return lax.ppermute(value, "tensor", route)


def over_all(value, target):
    sections, n_tensor, n_dp = (lax.axis_size(a) for a in ALL)
    route = []
    for s in range(sections):
        for t in range(n_tensor):
            for d in range(n_dp):
                ts, tt, td = target(s, t, d)
                if ts >= 0:
                    here = (s * n_tensor + t) * n_dp + d
                    route.append((here, (ts * n_tensor + tt) * n_dp + td))
    return lax.ppermute(value, ALL, route)


def swap_dp(value):
    return lax.ppermute(value, "dp", [(0, 1), (1, 0)])


def home_parts(value, dp_id, new_section, dy=0):
    own = value.shape[-1] // 2
    left, right = value[..., :own], value[..., own:]
    got = []
    for j in range(2):
        chosen = jnp.where(dp_id == j, left, right)

        def target(s, t, d, j=j):
            b = 2 * t + (j ^ d)
            return new_section(s), (b % 16) ^ (dy << 1), b // 16

        got.append(over_all(chosen, target))
    return got


def to_home(value, dp_id, t_id, new_section, dy=0):
    got = home_parts(value, dp_id, new_section, dy)
    even = t_id % 2 == 0
    return jnp.stack([jnp.where(even, got[0], got[1]), jnp.where(even, got[1], got[0])])


def from_home(value, dp_id, t_id, new_section):
    even = t_id % 2 == 0
    got = []
    for j in range(2):
        chosen = jnp.where(even, value[j], value[1 - j])

        def target(s, t, d, j=j):
            return new_section(s), (16 * d + t) // 2, j ^ (t % 2)

        got.append(over_all(chosen, target))
    first = dp_id == 0
    return jnp.concatenate(
        [jnp.where(first, got[0], got[1]), jnp.where(first, got[1], got[0])], axis=-1
    )


def call(kernel, arrays, specs, gates, mib=3, **settings):
    n = len(arrays)
    settings["compiler_params"] = pltpu.CompilerParams(vmem_limit_bytes=mib * 2**20)

    def body(*refs):
        kernel(*refs[:n], *refs[n + len(gates) :])

    specs = list(specs) + [pl.BlockSpec(memory_space=pl.ANY)] * len(gates)
    return pl.pallas_call(body, in_specs=specs, **settings)(*arrays, *gates)


VMEM = pl.BlockSpec(memory_space=pltpu.VMEM)
SMEM = pl.BlockSpec(memory_space=pltpu.SMEM)
ANY = pl.BlockSpec(memory_space=pl.ANY)


def cost(flops, bytes_accessed):
    return pl.CostEstimate(flops=flops, bytes_accessed=bytes_accessed, transcendentals=0)


def in_vmem(*arrays):
    return [pltpu.with_memory_space_constraint(a, pltpu.VMEM) for a in arrays]


def in_hbm(*arrays):
    return [pltpu.with_memory_space_constraint(a, pltpu.HBM) for a in arrays]


def given_kernel(core, u_ref, w_ref, u_out, w_out, sems):
    block = u_out.shape[0] // 8
    copies = []
    for ref, out in ((u_ref, u_out), (w_ref, w_out)):
        for i in range(8):
            start = pl.multiple_of((2 * i + 1 - core[0]) * block, block)
            copies.append(
                pltpu.make_async_copy(
                    ref.at[pl.ds(start, block)],
                    out.at[pl.ds(i * block, block)],
                    sems.at[len(copies)],
                )
            )
    for copy in copies:
        copy.start()
    for copy in copies:
        copy.wait()


def given(first, second, core):
    rows, cols = first.shape
    return call(
        given_kernel,
        [core, *in_hbm(first, second)],
        [SMEM, ANY, ANY],
        (),
        out_specs=[VMEM] * 2,
        out_shape=[pltpu.VMEM((rows // 2, cols), BF16)] * 2,
        scratch_shapes=[pltpu.SemaphoreType.DMA((16,))],
        mib=8,
        cost_estimate=cost(0, 4 * rows * cols),
    )


def sum_kernel(y, p_ref, a_ref, b_ref, c_ref, g_ref, o_ref):
    own = o_ref.shape[1] // 2
    total = p_ref[...].astype(F32) + a_ref[...].astype(F32)
    total += b_ref[...].astype(F32) + c_ref[...].astype(F32)
    mine = lax.broadcasted_iota(jnp.int32, total.shape, 1) // own == y[0]
    o_ref[...] = (total + jnp.where(mine, g_ref[...].astype(F32), 0)).astype(BF16)


def z_sum(piece, arrived, grad, y, gates):
    return call(
        sum_kernel,
        [y, *in_vmem(piece, *arrived, grad)],
        [SMEM] + [VMEM] * 5,
        gates,
        out_specs=VMEM,
        out_shape=pltpu.VMEM(piece.shape, BF16),
        cost_estimate=cost(6 * piece.size, 12 * piece.size),
    )


def enter_kernel(at, s_ref, a_ref, t_ref, o_ref, own_ref):
    own = own_ref.shape[1]
    total = (s_ref[...].astype(F32) + a_ref[...].astype(F32)).astype(BF16)
    own_ref[...] = jnp.where(at[0] == 0, total[:, :own], total[:, own:])
    o_ref[...] = jnp.where(at[1] == 1, t_ref[...], total)


def enter(straight, across, top, at, gates):
    rows, width = straight.shape
    return call(
        enter_kernel,
        [at, *in_vmem(straight, across, top)],
        [SMEM] + [VMEM] * 3,
        gates,
        out_specs=[VMEM] * 2,
        out_shape=[
            pltpu.VMEM((rows, width), BF16),
            pltpu.VMEM((rows, width // 2), BF16),
        ],
        cost_estimate=cost(2 * straight.size, 8 * straight.size),
    )


def outer_kernel(order, n0, n1, f0, f1, h_ref, o_ref, held, sems):
    own = n0.shape[1] // 8
    heads = h_ref[...]
    copies = []
    for i in range(16):
        at = slice(i % 8 * own, (i % 8 + 1) * own)
        block = [half[:, at] for half in ((n0, n1) if i < 8 else (f0, f1))]
        held[i] = lax.dot_general(
            jnp.concatenate(block, axis=0),
            heads,
            (((0,), (0,)), ((), ())),
            preferred_element_type=F32,
        ).astype(held.dtype)
        start = pl.multiple_of(order[i] * own, own)
        copy = pltpu.make_async_copy(held.at[i], o_ref.at[pl.ds(start, own)], sems.at[i])
        copy.start()
        copies.append(copy)
    for copy in copies:
        copy.wait()


def outer(near, far, heads, order):
    tokens, cols = heads.shape
    width = near[0].shape[1]
    own = width // 8
    return call(
        outer_kernel,
        [order, *near, *far, heads],
        [SMEM] + [VMEM] * 5,
        (),
        out_specs=ANY,
        out_shape=jax.ShapeDtypeStruct((2 * width, cols), BF16),
        scratch_shapes=[pltpu.VMEM((16, own, cols), BF16), pltpu.SemaphoreType.DMA((16,))],
        mib=10,
        cost_estimate=cost(4 * tokens * width * cols, 4 * (tokens * width + width * cols)),
    )


def slots_kernel(slots, held_ref, o_ref, sems):
    copies = [
        pltpu.make_async_copy(held_ref.at[slots[m]], o_ref.at[m], sems.at[m])
        for m in range(o_ref.shape[0])
    ]
    for copy in copies:
        copy.start()
    for copy in copies:
        copy.wait()


def in_slots(held, slots, gates):
    return call(
        slots_kernel,
        [slots, held],
        [SMEM, ANY],
        gates,
        out_specs=VMEM,
        out_shape=pltpu.VMEM(held.shape, BF16),
        scratch_shapes=[pltpu.SemaphoreType.DMA((held.shape[0],))],
        cost_estimate=cost(0, 4 * held.size),
    )


def stash_kernel(odd, a_ref, b_ref, o_ref):
    even = odd[0] == 0
    micro, seq, _ = a_ref.shape
    for m in range(micro):
        for r, (first, second) in enumerate(((a_ref, b_ref), (b_ref, a_ref))):
            at = slice((2 * m + r) * seq, (2 * m + r + 1) * seq)
            o_ref[at, :] = jnp.where(even, first[m], second[m])


def stash_rows(parts, odd, gates):
    micro, seq, own = parts[0].shape
    return call(
        stash_kernel,
        [odd, *parts],
        [SMEM] + [VMEM] * 2,
        gates,
        out_specs=VMEM,
        out_shape=jax.ShapeDtypeStruct((2 * micro * seq, own), BF16),
        cost_estimate=cost(0, 8 * parts[0].size),
    )


def tie_kernel(x_ref, o_ref):
    pass


def tie(value, *gates):
    return call(
        tie_kernel,
        [value],
        [ANY],
        gates,
        out_specs=ANY,
        out_shape=jax.ShapeDtypeStruct(value.shape, value.dtype),
        input_output_aliases={0: 0},
        cost_estimate=cost(0, 0),
    )


def probs_kernel(qk_ref, o_ref):
    micro, n_heads, seq, _ = o_ref.shape
    query = lax.broadcasted_iota(jnp.int32, (seq, seq), 0)
    key = lax.broadcasted_iota(jnp.int32, (seq, seq), 1)
    for m in range(micro):
        for h in range(n_heads):
            at = slice(h * DH, (h + 1) * DH)
            scores = lax.dot_general(
                qk_ref[m, 0, :, at],
                qk_ref[m, 1, :, at],
                (((1,), (1,)), ((), ())),
                preferred_element_type=F32,
            )
            scores = jnp.where(key <= query, scores * DH ** (-0.5), -jnp.inf)
            weights = jnp.exp(scores - jnp.max(scores, axis=-1, keepdims=True))
            weights = weights / jnp.sum(weights, axis=-1, keepdims=True)
            o_ref[m, h] = weights.astype(o_ref.dtype)


def attention_probs(query_key, gates):
    micro, _, seq, cols = query_key.shape
    return call(
        probs_kernel,
        [query_key],
        [VMEM],
        gates,
        out_specs=VMEM,
        out_shape=jax.ShapeDtypeStruct((micro, cols // DH, seq, seq), BF16),
        cost_estimate=cost(2 * micro * seq * seq * cols, 2 * query_key.size),
    )


def heads_kernel(turned, n_micro, position, mine_ref, there_ref, probs_ref, o_ref):
    total = (mine_ref[...].astype(F32) + there_ref[...].astype(F32)).astype(BF16)
    _, n_rep, n_heads, seq, _ = probs_ref.shape
    for m in range(n_micro):
        for r in range(n_rep):
            for h in range(n_heads):
                rows = slice((m * n_rep + r) * seq, (m * n_rep + r + 1) * seq)
                cols = slice(h * DH, (h + 1) * DH)
                o_ref[rows, cols] = lax.dot_general(
                    probs_ref[position[0] + m, r, h],
                    total[rows, cols],
                    (((0 if turned else 1,), (0,)), ((), ())),
                    preferred_element_type=F32,
                ).astype(o_ref.dtype)


def head_products(mine, there, probs, position, turned, gates):
    n_micro = mine.shape[0] // (probs.shape[1] * probs.shape[3])
    return call(
        functools.partial(heads_kernel, turned, n_micro),
        [position, *in_vmem(mine, there, probs)],
        [SMEM] + [VMEM] * 3,
        gates,
        out_specs=VMEM,
        out_shape=pltpu.VMEM(mine.shape, BF16),
        cost_estimate=cost(2 * mine.size * probs.shape[-1], 6 * mine.size),
    )


def weight_copies(order, own_ref, got_ref, held, sems):
    block = held.shape[1] // 2
    copies = []
    for k in range(NZ):
        group = []
        for y in range(2):
            t = order[2 * k + y]
            at = pl.ds(y * block, block)
            cols = own_ref.shape[1]
            own = own_ref.at[pl.ds(pl.multiple_of(t * block, block), block)]
            got = got_ref.at[pl.ds(pl.multiple_of(t // 2 * block, block), block)]
            sem = sems.at[2 * (2 * k + y)], sems.at[2 * (2 * k + y) + 1]
            group.append(pltpu.make_async_copy(own, held.at[k, at, pl.ds(0, cols)], sem[0]))
            group.append(pltpu.make_async_copy(got, held.at[k, at, pl.ds(cols, cols)], sem[1]))
        copies.append(group)
    return copies


def load_kernel(turned, order, own_ref, got_ref, o_ref, *scratch):
    held = scratch[0] if turned else o_ref
    copies = weight_copies(order, own_ref, got_ref, held, scratch[-1])
    for group in copies:
        for copy in group:
            copy.start()
    for k, group in enumerate(copies):
        for copy in group:
            copy.wait()
        if turned:
            o_ref[k] = held[k].T


def load(own, got, order, turned, gates):
    width, cols = own.shape[0] // (2 * NZ), 2 * own.shape[1]
    held = [pltpu.VMEM((NZ, width, cols), BF16)] if turned else []
    shape = (NZ, cols, width) if turned else (NZ, width, cols)
    return call(
        functools.partial(load_kernel, turned),
        [order, *in_hbm(own, got)],
        [SMEM, ANY, ANY],
        gates,
        out_specs=VMEM,
        out_shape=pltpu.VMEM(shape, BF16),
        scratch_shapes=held + [pltpu.SemaphoreType.DMA((4 * NZ,))],
        mib=11 if turned else 6,
        cost_estimate=cost(0, 8 * NZ * width * cols),
    )


def gather_kernel(a0, a1, a2, a3, w_ref, keep_ref, give_ref, total):
    cols = keep_ref.shape[1]
    for k, a in enumerate((a0, a1, a2, a3)):
        term = jnp.dot(a[...], w_ref[k], preferred_element_type=F32)
        if k == 0:
            total[...] = term
        elif k < NZ - 1:
            total[...] += term
        else:
            term = term + total[...]
            keep_ref[...] = term[:, :cols]
            give_ref[...] = term[:, cols:].astype(give_ref.dtype)


def gather_product(pieces, weights, gates):
    rows, width = pieces[0].shape
    cols = weights.shape[2] // 2
    return call(
        gather_kernel,
        in_vmem(*pieces, weights),
        [VMEM] * 5,
        gates,
        out_specs=[VMEM] * 2,
        out_shape=[pltpu.VMEM((rows, cols), F32), pltpu.VMEM((rows, cols), BF16)],
        scratch_shapes=[pltpu.VMEM((rows, 2 * cols), F32)],
        mib=3,
        cost_estimate=cost(16 * rows * width * cols, 16 * width * cols),
    )


def branch_kernel(v_ref, c_ref, w_ref, o0, o1, o2, o3):
    both = jnp.concatenate([v_ref[...], c_ref[...]], axis=1)
    for k, out in enumerate((o0, o1, o2, o3)):
        out[...] = jnp.dot(both, w_ref[k], preferred_element_type=F32).astype(BF16)


def branch_product(vals, vals_core, weights):
    rows, cols = vals.shape
    width = weights.shape[2]
    return call(
        branch_kernel,
        in_vmem(vals, vals_core, weights),
        [VMEM] * 3,
        (),
        out_specs=[VMEM] * 4,
        out_shape=[pltpu.VMEM((rows, width), BF16)] * 4,
        mib=3,
        cost_estimate=cost(16 * rows * width * cols, 16 * width * cols),
    )


def pick_kernel(section, *refs):
    grads, near_ref, sems = refs[:-2], *refs[-2:]
    n = sems.shape[0]
    sections = len(grads) // n
    width = grads[0].shape[1]
    for s in range(sections):

        @pl.when(section[0] == s)
        def _(s=s):
            copies = []
            for k in range(n):
                copies.append(
                    pltpu.make_async_copy(
                        grads[s * n + k], near_ref.at[:, pl.ds(k * width, width)], sems.at[k]
                    )
                )
            for copy in copies:
                copy.start()
            for copy in copies:
                copy.wait()


def pick(grads, section, gates, n=NZ, fresh=0):
    rows, width = grads[0][0].shape
    flat = [piece for entry in grads for piece in entry]
    flat = in_vmem(*flat[: fresh * n]) + in_hbm(*flat[fresh * n :])
    return call(
        pick_kernel,
        [section, *flat],
        [SMEM] + [VMEM] * (fresh * n) + [ANY] * (len(flat) - fresh * n),
        gates,
        out_specs=VMEM,
        out_shape=pltpu.VMEM((rows, n * width), BF16),
        scratch_shapes=[pltpu.SemaphoreType.DMA((n,))],
        cost_estimate=cost(0, 4 * rows * n * width),
    )


def pick_one(seen, section, gates, fresh=0):
    return pick([[one] for one in seen], section, gates, 1, fresh)


def dot(a, b):
    return jnp.dot(a, b, preferred_element_type=F32)


def on_device(held_input, query_key, w_value, w_out, grad_top, slot_table):
    sections = lax.axis_size("section")
    section_id = lax.axis_index("section")
    t_id = lax.axis_index("tensor")
    dp_id = lax.axis_index("dp")
    z, y, c = place(t_id)
    micro, seq, two_own = held_input.shape[2:]
    own = two_own // 2
    local_cols = w_value.shape[2]
    heads = local_cols // DH
    rows = 2 * seq
    lower = y == 0

    same, other = (to_home(grad_top[0], dp_id, t_id, lambda s: s, dy) for dy in range(2))
    pair = [jnp.where(lower, same, other), jnp.where(lower, other, same)]
    tops = jnp.swapaxes(jnp.concatenate(pair, axis=-1), 0, 1).reshape(micro, rows, two_own)
    top = tops[0]

    order = [index(z ^ k, yy, c) for k in range(NZ) for yy in range(2)]
    order = jnp.stack(order + [t ^ 1 for t in order]).astype(jnp.int32)

    core = c.astype(jnp.int32).reshape(1)
    section = section_id.astype(jnp.int32).reshape(1)
    at = jnp.stack([y, section_id == sections - 1]).astype(jnp.int32)

    out_given, value_given = given(w_out[0], w_value[0], core)
    out_got = in_group(out_given, dc=1)
    value_got = in_group(value_given, dc=1)

    probs = attention_probs(query_key[0, 0], (out_got,))
    probs_there = swap_dp(probs)
    first = dp_id == 0
    probs = jnp.stack(
        [jnp.where(first, probs, probs_there), jnp.where(first, probs_there, probs)], axis=1
    )

    tick_total = micro + sections - 1
    incoming = top
    out_ready = load(w_out[0], out_got, order, False, ())
    grads_seen, values_seen, inputs_seen = [], [], []
    stash = values = values_there = heads_out = layer_in = None

    def chosen(seen):
        return lax.select_n(section_id, *seen)

    for tick in range(tick_total):
        last = tick == tick_total - 1
        position = jnp.clip(tick - (sections - 1 - section_id), 0, micro - 1)
        position = position.astype(jnp.int32).reshape(1)
        near = {k: in_group(incoming, dz=k) for k in (2, 1, 3)}
        near = [incoming] + [near[k] for k in range(1, NZ)]
        grads_seen.append(near)
        gates = ()
        if tick == 1:
            stash = stash_rows(stash, c.astype(jnp.int32).reshape(1), (incoming,))
            layer_in = lax.all_gather(stash, "tensor", axis=1, tiled=True)
        if last:
            first_grads = pick(grads_seen[:sections][::-1], section, (incoming,))
            ends = [
                pick_one(
                    [
                        inputs_seen[min(sections - 1 - (s + 1) % sections + m, tick - 1)]
                        for s in range(sections)
                    ],
                    section,
                    (incoming,),
                )
                for m in range(micro)
            ]
            early = from_home(
                jnp.stack([end.reshape(2, seq, own) for end in ends], axis=1),
                dp_id,
                t_id,
                lambda s: (s + 1) % sections,
            )
            first_values = pick_one(values_seen[::-1], section, (incoming,))
            gates = (first_grads, first_values, *ends)
        keep, give = gather_product(near, out_ready, gates)
        from_core = in_group(give, dc=1)
        grad_heads = (keep + from_core.astype(F32)).astype(BF16)
        there = swap_dp(grad_heads)
        value_ready = load(w_value[0], value_got, order, True, (grad_heads,))
        gates = (value_ready,)
        if tick == 3:
            heads_out = head_products(
                values, values_there, probs, jnp.zeros((1,), jnp.int32), False, (grad_heads,)
            )
            gates += (heads_out,)
        if last:
            later_grads = pick(grads_seen[1:][::-1], section, (grad_heads,), fresh=1)
            gates += (later_grads,)
        grad_vals = head_products(grad_heads, there, probs, position, True, gates)
        values_seen.append(grad_vals)
        pieces = branch_product(grad_vals, in_group(grad_vals, dc=1), value_ready)
        arrived = [in_group(pieces[k], dz=k) for k in (2, 1, 3)]
        gates = ()
        if last:
            far = [
                in_group(tie(picked, pieces[0]), dc=1) for picked in (first_grads, later_grads)
            ]
            grad_w_out = outer([first_grads, later_grads], far, heads_out, order)
            later_values = pick_one(values_seen[1:][::-1], section, (pieces[0],), 1)
            grad_w_value = lax.dot_general(
                layer_in,
                jnp.concatenate([first_values, later_values], axis=0),
                (((0,), (0,)), ((), ())),
                preferred_element_type=F32,
            ).astype(BF16)
            gates = (grad_w_value, *in_hbm(grad_w_out))
        sent = z_sum(pieces[0], arrived, incoming, at[:1], gates)
        if tick == 0:
            slot_row = lax.dynamic_index_in_dim(
                slot_table, sections - 1 - section_id, 0, keepdims=False
            )
            ordered = in_slots(held_input[0, 0], slot_row, (sent,))
            stash = home_parts(ordered, dp_id, lambda s: sections - 1 - s)
        if last:
            across = in_group(sent, dy=1)
            _, done = enter(sent, across, sent, at, ())
        else:
            across = over_all(sent, lambda s, t, d: ((s - 1) % sections, t ^ 2, d))
            straight = over_all(sent, lambda s, t, d: ((s - 1) % sections, t, d))
            out_ready = load(w_out[0], out_got, order, False, (sent,))
            gates = ()
            if tick == 2:
                values = dot(layer_in, w_value[0]).astype(BF16)
                values_there = swap_dp(values)
                gates = (values,)
            incoming, completed = enter(straight, across, tops[1], at, gates)
            inputs_seen.append(completed)

    late = from_home(done.reshape(2, seq, own), dp_id, t_id, lambda s: s if s == 0 else -1)
    late = jnp.where(section_id == 0, late, early[micro - 1])
    grad_input = jnp.stack([*early[: micro - 1], late])
    return grad_input[None, None], grad_w_value[None], grad_w_out[None]


def solution(mesh):
    return jax.shard_map(
        on_device,
        mesh=mesh,
        in_specs=(
            P("section", "dp", None, None, "tensor"),
            P("section", "dp", None, None, None, "tensor"),
            P("section", "dp", "tensor"),
            P("section", "dp", "tensor"),
            P("dp", None, None, "tensor"),
            P(),
        ),
        out_specs=(
            P("section", "dp", None, None, "tensor"),
            P("section", "dp", "tensor"),
            P("section", "dp", "tensor"),
        ),
        check_vma=False,
    )
```
